32 devices in a mesh: gx: 8 (over z, core), gy: 4 (over y, x).
Axes of the slice: x: 2, y: 2, z: 4, core: 2. Of those that a mesh axis runs over, the one named last changes fastest.
Arguments:
- source: float32 [2, 256, 1024], P(None, 'gx', 'gy'), may hold values from -8 to 8
- coef_x: float32 [2, 256, 1024], P(None, 'gx', 'gy'), may hold values from 0.2 to 5
- coef_y: float32 [2, 256, 1024], P(None, 'gx', 'gy'), may hold values from 0.2 to 5
- coef_z: float32 [256, 1024], P('gx', 'gy'), may hold values from 1 to 20
- surface: float32 [2, 256, 1024], P(None, 'gx', 'gy'), may hold values from 0.05 to 0.5
Outputs:
- pressure: float32 [2, 256, 1024], P(None, 'gx', 'gy')
- residual: float32 [2, 256, 1024], P(None, 'gx', 'gy')
The draws below stay inside these ranges and needn't reach their ends.
All inputs are finite; a program needn't handle non-finite values.
Results may differ from the reference program's by a relative error of at most 0.0003.
Values sent between devices are 32-bit elements; how exact they have to be, the bound alone decides.
No kernel may reach another device: no remote copies, remote signals or barrier semaphores. Data moves between devices by JAX's collectives and lax.ppermute only.
A program may use at most 64 MiB of HBM per device.

```python
import math
import jax
import jax.numpy as jnp

LAYERS = 2
LEVELS = 4
PRE = 2
POST = 2
CSWEEPS = 8
NX = 256
NY = 1024


def draw_source(key, part):
    values = jax.random.normal(key, (LAYERS, NX, NY), jnp.float32)
    values = values + 0.5
    return jnp.clip(values, -8.0, 8.0)


def block_scale(rng, extent, shards, least, largest):
    loudness, own = 1.0, jax.random.fold_in(rng, 6)
    for axis_at, shards_of in shards:
        steps = jnp.exp(jax.random.uniform(jax.random.fold_in(own, axis_at), (shards_of,), jnp.float32, least / len(shards), largest / len(shards)))
        loudness = loudness * jnp.repeat(steps, extent[axis_at] // shards_of).reshape([-1 if axis == axis_at else 1 for axis in range(len(extent))])
    return loudness


def setup_inputs(seed: int = 0) -> dict:
    arg_keys = jax.random.split(jax.random.key(seed), 6)
    return {
        "source": draw_source(jax.random.fold_in(arg_keys[5], 71), 0),
        "coef_x": jnp.clip(jnp.exp(math.log(5.0) - 3.218876 * jax.random.uniform(arg_keys[1], (LAYERS, NX, NY), jnp.float32) ** block_scale(arg_keys[1], (LAYERS, NX, NY), ((1, 8), (2, 4)), -0.2, 0.2)), 0.2, 5.0),
        "coef_y": jnp.clip(jnp.exp(math.log(5.0) - 3.218876 * jax.random.uniform(arg_keys[2], (LAYERS, NX, NY), jnp.float32) ** block_scale(arg_keys[2], (LAYERS, NX, NY), ((1, 8), (2, 4)), -0.2, 0.2)), 0.2, 5.0),
        "coef_z": jnp.clip(jnp.exp(math.log(20.0) - 2.9957323 * jax.random.uniform(arg_keys[3], (NX, NY), jnp.float32) ** block_scale(arg_keys[3], (NX, NY), ((0, 8), (1, 4)), -0.2, 0.2)), 1.0, 20.0),
        "surface": jnp.clip(jnp.exp(math.log(0.5) - 2.3025851 * jax.random.uniform(arg_keys[4], (LAYERS, NX, NY), jnp.float32) ** block_scale(arg_keys[4], (LAYERS, NX, NY), ((1, 8), (2, 4)), -0.2, 0.2)), 0.05, 0.5),
    }


damping = 0.8


def operate(u_ext, kx_ext, ky_ext, kz, surf):
    u = u_ext[:, 1:-1, 1:-1]
    kx_hi = kx_ext[:, 1:, :]
    kx_lo = kx_ext[:, :-1, :]
    ky_hi = ky_ext[:, :, 1:]
    ky_lo = ky_ext[:, :, :-1]
    vert = kz * (u[0] - u[1])
    result = surf * u + kx_hi * (u - u_ext[:, 2:, 1:-1]) + kx_lo * (u - u_ext[:, :-2, 1:-1])
    result = result + ky_hi * (u - u_ext[:, 1:-1, 2:]) + ky_lo * (u - u_ext[:, 1:-1, :-2])
    return result + jnp.stack([vert, -vert])


def diagonal(kx_ext, ky_ext, kz, surf):
    return surf + kx_ext[:, 1:, :] + kx_ext[:, :-1, :] + ky_ext[:, :, 1:] + ky_ext[:, :, :-1] + kz[None]


def coarsen(kx, ky, kz, surf):
    kx_c = kx[:, 1::2, 0::2] + kx[:, 1::2, 1::2]
    ky_c = ky[:, 0::2, 1::2] + ky[:, 1::2, 1::2]
    kz_c = kz[0::2, 0::2] + kz[1::2, 0::2] + kz[0::2, 1::2] + kz[1::2, 1::2]
    s_c = surf[:, 0::2, 0::2] + surf[:, 1::2, 0::2] + surf[:, 0::2, 1::2] + surf[:, 1::2, 1::2]
    return kx_c, ky_c, kz_c, s_c


def restrict(field):
    return field[:, 0::2, 0::2] + field[:, 1::2, 0::2] + field[:, 0::2, 1::2] + field[:, 1::2, 1::2]


def prolong(field):
    return jnp.repeat(jnp.repeat(field, 2, axis=1), 2, axis=2)


def extend(u):
    return jnp.pad(u, ((0, 0), (1, 1), (1, 1)))


def sweeps(level, rhs_now, count):
    kx_ext, ky_ext, kz, surf = level
    diag = diagonal(kx_ext, ky_ext, kz, surf)
    u = damping * rhs_now / diag
    for step in range(count - 1):
        u = u + damping * (rhs_now - operate(extend(u), kx_ext, ky_ext, kz, surf)) / diag
    return u, diag


def cycle(levels, depth, rhs_now):
    if depth == LEVELS:
        kx_ext, ky_ext, kz, surf = levels[depth]
        coarse_u = sweeps(levels[depth], rhs_now, CSWEEPS)[0]
        coarse_r = rhs_now - operate(extend(coarse_u), kx_ext, ky_ext, kz, surf)
        return coarse_u + jnp.sum(coarse_r) / jnp.sum(surf)
    kx_ext, ky_ext, kz, surf = levels[depth]
    u, diag = sweeps(levels[depth], rhs_now, PRE)
    resid = rhs_now - operate(extend(u), kx_ext, ky_ext, kz, surf)
    u = u + prolong(cycle(levels, depth + 1, restrict(resid)))
    for step in range(POST):
        u = u + damping * (rhs_now - operate(extend(u), kx_ext, ky_ext, kz, surf)) / diag
    return u


def reference(source, coef_x, coef_y, coef_z, surface):
    kx = coef_x.at[:, -1, :].set(0.0)
    ky = coef_y.at[:, :, -1].set(0.0)
    kz, surf = coef_z, surface
    levels = []
    for depth in range(LEVELS + 1):
        kx_ext = jnp.pad(kx, ((0, 0), (1, 0), (0, 0)))
        ky_ext = jnp.pad(ky, ((0, 0), (0, 0), (1, 0)))
        levels.append((kx_ext, ky_ext, kz, surf))
        if depth < LEVELS:
            kx, ky, kz, surf = coarsen(kx, ky, kz, surf)
    pressure = cycle(levels, 0, source)
    kx_ext, ky_ext, kz, surf = levels[0]
    residual = source - operate(extend(pressure), kx_ext, ky_ext, kz, surf)
    return pressure, residual
```

```python
import functools

import jax
import jax.numpy as jnp
from jax import lax
from jax.experimental import pallas as pl
from jax.experimental.pallas import tpu as pltpu
from jax.sharding import PartitionSpec as P

LEVELS = 4
PRE = 2
POST = 2
CSWEEPS = 8
damping = 0.8

LANES = 128
WIDTH = 28
PAD = 8
PLANES = 9
F, KX, KY, S, KZ = 0, 2, 4, 6, 8
W, U = 9, 11


def pair_permute(x, axis, first):
    count = lax.axis_size(axis)
    pairs = []
    for i in range(first, count - 1, 2):
        pairs += [(i, i + 1), (i + 1, i)]
    return lax.ppermute(x, axis, pairs)


def lane_iota(shape):
    return lax.broadcasted_iota(jnp.int32, shape, len(shape) - 1)


def from_right(x, step):
    rolled = pltpu.roll(x, LANES - step, x.ndim - 1)
    if x.shape[1] == 1:
        return rolled
    after = jnp.concatenate([rolled[:, 1:], rolled[:, :1]], axis=1)
    return jnp.where(lane_iota(x.shape) >= LANES - step, after, rolled)


def from_left(x, step):
    rolled = pltpu.roll(x, step, x.ndim - 1)
    if x.shape[1] == 1:
        return rolled
    before = jnp.concatenate([rolled[:, -1:], rolled[:, :-1]], axis=1)
    return jnp.where(lane_iota(x.shape) < step, before, rolled)


def weight(kx, kx_lo, ky, kz, surf, step):
    diag = surf + kx + kx_lo + ky + from_left(ky, step) + kz
    return jnp.where(diag > 0.0, damping / jnp.where(diag > 0.0, diag, 1.0), 0.0)


def residual_of(f, u, u_up, u_dn, kx, kx_lo, ky, kz, surf, step):
    flux = ky * (u - from_right(u, step))
    vert = kz * (u[0:1] - u[1:2])
    out = surf * u + kx * (u - u_up) + kx_lo * (u - u_dn)
    out = out + flux - from_left(flux, step)
    return f - (out + jnp.concatenate([vert, -vert], axis=0))


def rows_of(ref, plane, count, start, size=8):
    return ref[plane : plane + count, :, start : start + size, :]


def block_residual(level, u_ref, u_at, step, r0):
    u = rows_of(u_ref, u_at, 2, r0)
    return u, residual_of(
        rows_of(level, F, 2, r0),
        u,
        rows_of(u_ref, u_at, 2, r0 + 1),
        rows_of(u_ref, u_at, 2, r0 - 1),
        rows_of(level, KX, 2, r0),
        rows_of(level, KX, 2, r0 - 1),
        rows_of(level, KY, 2, r0),
        rows_of(level, KZ, 1, r0),
        rows_of(level, S, 2, r0),
        step,
    )


def put(ref, plane, r0, value):
    ref[plane : plane + value.shape[0], :, r0 : r0 + value.shape[2], :] = value


def strided(ref, plane, count, start, size):
    tiles = ref.shape[1]
    return jnp.stack(
        [
            jnp.stack([ref[plane + p, c, pl.ds(start, size, stride=2), :] for c in range(tiles)])
            for p in range(count)
        ]
    )


def put_strided(ref, plane, start, value):
    for p in range(value.shape[0]):
        for c in range(value.shape[1]):
            ref[plane + p, c, pl.ds(start, value.shape[2], stride=2), :] = value[p, c]


def zero_pads(ref, planes):
    rows = ref.shape[2]
    for plane in planes:
        zero = jnp.zeros((1, ref.shape[1], PAD, LANES), jnp.float32)
        put(ref, plane, 0, zero)
        put(ref, plane, rows - PAD, zero)


def coarse_block(fine, resid, step, fine_row, size):
    def both(ref, plane, count):
        return strided(ref, plane, count, fine_row, size) + strided(
            ref, plane, count, fine_row + 1, size
        )

    f = both(resid, 0, 2)
    kx = strided(fine, KX, 2, fine_row + 1, size)
    ky = both(fine, KY, 2)
    surf_kz = both(fine, S, 3)
    summed = jnp.concatenate([f, kx, surf_kz], axis=0)
    summed = summed + from_right(summed, step)
    return summed[0:2], summed[2:4], from_right(ky, step), summed[4:7]


def sides(mine, other, is_even):
    low = jnp.where(is_even, other, mine)
    high = jnp.where(is_even, mine, other)
    return low, high


def strip_kernel(own_ref, near_ref, far_ref, c_ref, d_ref):
    even_x = lax.rem(lax.axis_index("gx"), 2) == 0
    even_y = lax.rem(lax.axis_index("gy"), 2) == 0
    rows = own_ref.shape[1]
    cols = own_ref.shape[2]
    lane = lane_iota((8, LANES))

    def place(pieces, offset):
        tiles = [jnp.zeros((8, LANES), jnp.float32)] * 2
        for p in range(PLANES):
            begin = p * WIDTH
            rolled = pltpu.roll(pieces[p], (begin - offset) % LANES, 1)
            for a in range(2):
                lo, hi = begin - a * LANES, begin + WIDTH - a * LANES
                if hi > 0 and lo < LANES:
                    tiles[a] = jnp.where((lane >= lo) & (lane < hi), rolled, tiles[a])
        return tiles

    for block in range(3 * rows // 8):
        part, r0 = divmod(block * 8, rows)
        first, last = [], []
        for p in range(PLANES):
            for held, column in ((first, 0), (last, cols - LANES)):
                at = (p, slice(r0, r0 + 8), slice(column, column + LANES))
                if part == 1:
                    held.append(own_ref[at])
                else:
                    held.append(sides(near_ref[at], far_ref[at], even_x)[part // 2])
        left = place(first, 0)
        right = place(last, LANES - WIDTH)
        for a in range(2):
            at = (slice(block * 8, block * 8 + 8), slice(a * LANES, (a + 1) * LANES))
            c_ref[at] = jnp.where(even_y, right[a], left[a])
            d_ref[at] = jnp.where(even_y, left[a], right[a])


def down_kernel(own_ref, near_ref, far_ref, c_ref, d_ref, l0, l1, l2, pack_ref, ua, rr):
    even_x = lax.rem(lax.axis_index("gx"), 2) == 0
    even_y = lax.rem(lax.axis_index("gy"), 2) == 0
    rows = own_ref.shape[1]
    lane = lane_iota((8, LANES))

    def take(tiles, p, offset):
        begin = p * WIDTH
        a, b = begin // LANES, (begin + WIDTH - 1) // LANES
        piece = tiles[a]
        if a != b:
            piece = jnp.where(lane < begin + WIDTH - b * LANES, tiles[b], tiles[a])
        return pltpu.roll(piece, (offset - begin) % LANES, 1)

    for block in range(3 * rows // 8):
        part, r0 = divmod(block * 8, rows)
        to = slice(PAD + block * 8, PAD + block * 8 + 8)
        for p in range(PLANES):
            for c in range(2):
                at = (p, slice(r0, r0 + 8), slice(c * LANES, (c + 1) * LANES))
                if part == 1:
                    l0[p, c, to, :] = own_ref[at]
                else:
                    l0[p, c, to, :] = sides(near_ref[at], far_ref[at], even_x)[part // 2]
        low, high = [], []
        for a in range(2):
            at = (slice(block * 8, block * 8 + 8), slice(a * LANES, (a + 1) * LANES))
            lo, hi = sides(c_ref[at], d_ref[at], even_y)
            low.append(lo)
            high.append(hi)
        for p in range(PLANES):
            right = take(high, p, 0)
            left = take(low, p, LANES - WIDTH)
            l0[p, 2, to, :] = jnp.where(
                lane < WIDTH, right, jnp.where(lane >= LANES - WIDTH, left, 0.0)
            )

    for ref in (l0, l1, l2):
        zero_pads(ref, (KX, KX + 1, U, U + 1))
    for ref in (ua,):
        zero_pads(ref, (0, 1))

    levels = (l0, l1, l2)
    for depth, level in enumerate(levels):
        step = 1 << depth
        count = level.shape[2] - 2 * PAD
        starts = range(PAD, PAD + count, 8)
        if depth:
            for r0 in starts:
                f, kx, ky, surf_kz = coarse_block(
                    levels[depth - 1], rr, step // 2, PAD + 2 * (r0 - PAD), 8
                )
                put(level, F, r0, f)
                put(level, KX, r0, kx)
                put(level, KY, r0, ky)
                put(level, S, r0, surf_kz)
            if count * 2 + 2 * PAD > 0:
                put(ua, 0, PAD + count, jnp.zeros((2, 3, PAD, LANES), jnp.float32))
        for r0 in starts:
            w = weight(
                rows_of(level, KX, 2, r0),
                rows_of(level, KX, 2, r0 - 1),
                rows_of(level, KY, 2, r0),
                rows_of(level, KZ, 1, r0),
                rows_of(level, S, 2, r0),
                step,
            )
            put(level, W, r0, w)
            put(ua, 0, r0, w * rows_of(level, F, 2, r0))
        for r0 in starts:
            u, r = block_residual(level, ua, 0, step, r0)
            put(level, U, r0, u + rows_of(level, W, 2, r0) * r)
        for r0 in starts:
            put(rr, 0, r0, block_residual(level, level, U, step, r0)[1])

    own = l2.shape[2] // 2 - 4
    f, kx, ky, surf_kz = coarse_block(l2, rr, 4, own, 4)
    nine = jnp.concatenate([f, kx, ky, surf_kz], axis=0)
    total = jnp.zeros((PLANES, LANES), jnp.float32)
    for r in range(4):
        for c in range(2):
            src = lax.broadcasted_iota(jnp.int32, (LANES, LANES), 0) + c * LANES
            dst = lax.broadcasted_iota(jnp.int32, (LANES, LANES), 1) - r * 32
            pick = jnp.where((src == dst * 8) & (dst >= 0) & (dst < 32), 1.0, 0.0)
            total = total + jnp.dot(
                nine[:, c, r, :],
                pick,
                precision=lax.Precision.HIGHEST,
                preferred_element_type=jnp.float32,
            )
    pack_ref[...] = total


def whole_sweep(level, u, weights, step):
    f, kx, kx_lo, ky, kz, surf = level
    rows = u.shape[2]
    r = residual_of(
        f, u, pltpu.roll(u, rows - 1, 2), pltpu.roll(u, 1, 2), kx, kx_lo, ky, kz, surf, step
    )
    return u + weights * r, r


def up_kernel(nx, ny, x_ref, l0, l1, l2, p_ref, r_ref, g3, g4, ub, uc):
    me_x = lax.axis_index("gx")
    me_y = lax.axis_index("gy")
    tiles = ny // 4
    rows3 = nx * 4

    lane = lane_iota((rows3, LANES))
    row = lax.broadcasted_iota(jnp.int32, (rows3, LANES), 0)
    for p in range(PLANES):
        for q in range(tiles):
            if tiles == 1:
                x = x_ref[pl.ds(p, rows3, stride=PLANES), :]
            else:
                x = jnp.concatenate(
                    [
                        x_ref[pl.ds((i * ny + 4 * q) * PLANES + p, 4, stride=PLANES), :]
                        for i in range(nx)
                    ],
                    axis=0,
                )
            out = x
            for delta in range(-3, 4):
                if delta == 0:
                    continue
                moved = pltpu.roll(x, (-delta) % rows3, 0)
                moved = pltpu.roll(moved, (32 * delta) % LANES, 1)
                out = jnp.where(lane // 32 - row % 4 == delta, moved, out)
            g3[p, q, :, :] = out

    def gathered(ref):
        kx = ref[KX : KX + 2]
        return (
            ref[F : F + 2],
            kx,
            pltpu.roll(kx, 1, 2),
            ref[KY : KY + 2],
            ref[KZ : KZ + 1],
            ref[S : S + 2],
        )

    level3 = gathered(g3)
    w3 = weight(*level3[1:], 1)
    u3 = w3 * level3[0]
    u3, unused = whole_sweep(level3, u3, w3, 1)
    unused, r3 = whole_sweep(level3, u3, w3, 1)
    g4[0:2] = r3
    f, kx, ky, surf_kz = coarse_block(g3, g4, 1, 0, rows3 // 2)
    level4 = (f, kx, pltpu.roll(kx, 1, 2), ky, surf_kz[2:3], surf_kz[0:2])
    w4 = weight(*level4[1:], 2)
    u4 = w4 * f
    for step in range(CSWEEPS - 1):
        u4, unused = whole_sweep(level4, u4, w4, 2)
    unused, rc = whole_sweep(level4, u4, w4, 2)
    even = lane_iota(u4.shape) % 2 == 0

    def total(x):
        x = jnp.sum(jnp.where(even, x, 0.0), axis=(0, 1))
        return jnp.sum(jnp.sum(x, axis=0, keepdims=True), axis=1, keepdims=True)

    e4 = u4 + (total(rc) / total(level4[5]))[None, None]
    e4 = jnp.where(even, e4, from_left(e4, 1))
    put_strided(g4, 0, 0, e4)
    put_strided(g4, 0, 1, e4)
    u3 = u3 + g4[0:2]
    for step in range(POST):
        u3, unused = whole_sweep(level3, u3, w3, 1)

    rows2 = l2.shape[2] - 2 * PAD
    to_row = lax.broadcasted_iota(jnp.int32, (rows2, rows3), 0) // 2 - 4 + me_x * 4
    pick_row = jnp.where(
        to_row == lax.broadcasted_iota(jnp.int32, (rows2, rows3), 1), 1.0, 0.0
    )
    dot = functools.partial(
        jnp.dot, precision=lax.Precision.HIGHEST, preferred_element_type=jnp.float32
    )
    near = [[dot(pick_row, u3[k, q]) for q in range(tiles)] for k in range(2)]
    near = [jnp.concatenate([near[k][q] for k in range(2)], axis=0) for q in range(tiles)]
    for c in range(3):
        spread = jnp.zeros((2 * rows2, LANES), jnp.float32)
        for q in range(tiles):
            column = lax.broadcasted_iota(jnp.int32, (LANES, LANES), 1) + c * LANES
            column = jnp.where(column >= 320, column - 384, column)
            coarse = (column + 64) // 8 - 8 + me_y * 32 - q * LANES
            pick = jnp.where(
                coarse == lax.broadcasted_iota(jnp.int32, (LANES, LANES), 0), 1.0, 0.0
            )
            spread = spread + dot(near[q], pick)
        for k in range(2):
            uc[k, c, PAD : PAD + rows2, :] = spread[k * rows2 : (k + 1) * rows2]

    levels = (l0, l1, l2)
    zeros = jnp.zeros((2, 3, PAD, LANES), jnp.float32)
    for depth in (2, 1, 0):
        level = levels[depth]
        step = 1 << depth
        count = level.shape[2] - 2 * PAD
        margin = (24, 8, 0)[depth]
        starts = range(PAD + margin, PAD + count - margin, 8)
        for r0 in starts:
            put(uc, 0, r0, rows_of(uc, 0, 2, r0) + rows_of(level, U, 2, r0))
        for buf in (uc, ub):
            put(buf, 0, PAD + margin - 8, zeros)
            put(buf, 0, PAD + count - margin, zeros)
        for source, target in ((uc, ub), (ub, uc)):
            for r0 in starts:
                u, r = block_residual(level, source, 0, step, r0)
                put(target, 0, r0, u + rows_of(level, W, 2, r0) * r)
        if depth:
            finer = levels[depth - 1]
            need = (24, 8, 0)[depth - 1]
            half = step // 2
            first, last = need // 2, (finer.shape[2] - 2 * PAD - need) // 2
            blocks = []
            for r0 in range(first, last, 4):
                e = rows_of(uc, 0, 2, PAD + r0, 4)
                blocks.append(
                    jnp.where(lane_iota(e.shape) % step < half, e, from_left(e, half))
                )
            for r0, e in zip(range(first, last, 4), blocks):
                put_strided(ub, 0, PAD + 2 * r0, e)
                put_strided(ub, 0, PAD + 2 * r0 + 1, e)
            for r0 in range(PAD + need, PAD + 2 * last, 8):
                put(uc, 0, r0, rows_of(ub, 0, 2, r0))
        else:
            own = p_ref.shape[1]
            for r0 in range(0, own, 8):
                at = PAD + count // 2 - own // 2 + r0
                u, r = block_residual(level, uc, 0, step, at)
                for c in range(2):
                    p_ref[:, r0 : r0 + 8, c * LANES : (c + 1) * LANES] = u[:, c]
                    r_ref[:, r0 : r0 + 8, c * LANES : (c + 1) * LANES] = r[:, c]


def shape_of(*shape):
    return jax.ShapeDtypeStruct(shape, jnp.float32)


def vmem(*shape):
    return pltpu.VMEM(shape, jnp.float32)


def on_device(source, coef_x, coef_y, coef_z, surface):
    rows, cols = source.shape[1], source.shape[2]
    nx, ny = lax.axis_size("gx"), lax.axis_size("gy")
    row = lax.broadcasted_iota(jnp.int32, (1, rows, 1), 1)
    col = lax.broadcasted_iota(jnp.int32, (1, 1, cols), 2)
    last_row = jnp.where(lax.axis_index("gx") == nx - 1, rows - 1, -1)
    last_col = jnp.where(lax.axis_index("gy") == ny - 1, cols - 1, -1)
    kx = jnp.where(row == last_row, 0.0, coef_x)
    ky = jnp.where(col == last_col, 0.0, coef_y)
    packed = jnp.concatenate([source, kx, ky, surface, coef_z[None]], axis=0)

    near = pair_permute(packed, "gx", 0)
    far = pair_permute(packed, "gx", 1)
    params = pltpu.CompilerParams(vmem_limit_bytes=48 * 1024 * 1024)
    strips = pl.pallas_call(
        strip_kernel,
        out_shape=(shape_of(3 * rows, 2 * LANES),) * 2,
        compiler_params=params,
        name="strips",
    )(packed, near, far)
    strip_c = pair_permute(strips[0], "gy", 0)
    strip_d = pair_permute(strips[1], "gy", 1)

    heights = [3 * rows // (1 << depth) + 2 * PAD for depth in range(3)]
    planes = U + 2
    l0, l1, l2, pack = pl.pallas_call(
        down_kernel,
        out_shape=tuple(shape_of(planes, 3, h, LANES) for h in heights)
        + (shape_of(PLANES, LANES),),
        scratch_shapes=[vmem(2, 3, heights[0], LANES)] * 2,
        compiler_params=params,
        name="down",
    )(packed, near, far, strip_c, strip_d)

    devices = nx * ny
    everyone = lax.all_to_all(
        jnp.broadcast_to(pack[None], (devices, PLANES, LANES)), ("gx", "gy"), 0, 0, tiled=True
    ).reshape(devices * PLANES, LANES)

    tiles = ny // 4
    pressure, residual = pl.pallas_call(
        functools.partial(up_kernel, nx, ny),
        out_shape=(shape_of(*source.shape),) * 2,
        scratch_shapes=[
            vmem(PLANES, tiles, nx * 4, LANES),
            vmem(2, tiles, nx * 4, LANES),
            vmem(2, 3, heights[0], LANES),
            vmem(2, 3, heights[0], LANES),
        ],
        compiler_params=params,
        name="up",
    )(everyone, l0, l1, l2)
    return pressure, residual


def solution(mesh):
    layered, plane = P(None, "gx", "gy"), P("gx", "gy")
    return jax.shard_map(
        on_device,
        mesh=mesh,
        in_specs=(layered, layered, layered, plane, layered),
        out_specs=(layered, layered),
        check_vma=False,
    )
```

```python
import functools

import jax
import jax.numpy as jnp
from jax import lax
from jax.experimental import pallas as pl
from jax.experimental.pallas import tpu as pltpu
from jax.sharding import PartitionSpec as P

LEVELS = 4
PRE = 2
POST = 2
CSWEEPS = 8
damping = 0.8

LANES = 128
WIDTH = 28
PAD = 8
PLANES = 9
PACK = 16
F, KX, KY, S, KZ = 0, 2, 4, 6, 8
W, U = 9, 11


def pair_permute(x, axis, first):
    count = lax.axis_size(axis)
    pairs = []
    for i in range(first, count - 1, 2):
        pairs += [(i, i + 1), (i + 1, i)]
    return lax.ppermute(x, axis, pairs)


def lane_iota(shape):
    return lax.broadcasted_iota(jnp.int32, shape, len(shape) - 1)


def from_right(x, step):
    rolled = pltpu.roll(x, LANES - step, x.ndim - 1)
    if x.shape[1] == 1:
        return rolled
    after = jnp.concatenate([rolled[:, 1:], rolled[:, :1]], axis=1)
    return jnp.where(lane_iota(x.shape) >= LANES - step, after, rolled)


def from_left(x, step):
    rolled = pltpu.roll(x, step, x.ndim - 1)
    if x.shape[1] == 1:
        return rolled
    before = jnp.concatenate([rolled[:, -1:], rolled[:, :-1]], axis=1)
    return jnp.where(lane_iota(x.shape) < step, before, rolled)


def weight(kx, kx_lo, ky, kz, surf, step):
    diag = surf + kx + kx_lo + ky + from_left(ky, step) + kz
    return jnp.where(diag > 0.0, damping / jnp.where(diag > 0.0, diag, 1.0), 0.0)


def residual_of(f, u, u_up, u_dn, kx, kx_lo, ky, kz, surf, step):
    flux = ky * (u - from_right(u, step))
    vert = kz * (u[0:1] - u[1:2])
    out = surf * u + kx * (u - u_up) + kx_lo * (u - u_dn)
    out = out + flux - from_left(flux, step)
    return f - (out + jnp.concatenate([vert, -vert], axis=0))


def rows_of(ref, plane, count, start, size=8):
    return ref[plane : plane + count, :, start : start + size, :]


def block_residual(level, u_ref, u_at, step, r0):
    u = rows_of(u_ref, u_at, 2, r0)
    return u, residual_of(
        rows_of(level, F, 2, r0),
        u,
        rows_of(u_ref, u_at, 2, r0 + 1),
        rows_of(u_ref, u_at, 2, r0 - 1),
        rows_of(level, KX, 2, r0),
        rows_of(level, KX, 2, r0 - 1),
        rows_of(level, KY, 2, r0),
        rows_of(level, KZ, 1, r0),
        rows_of(level, S, 2, r0),
        step,
    )


def put(ref, plane, r0, value):
    ref[plane : plane + value.shape[0], :, r0 : r0 + value.shape[2], :] = value


def strided(ref, plane, count, start, size):
    tiles = ref.shape[1]
    return jnp.stack(
        [
            jnp.stack([ref[plane + p, c, pl.ds(start, size, stride=2), :] for c in range(tiles)])
            for p in range(count)
        ]
    )


def put_strided(ref, plane, start, value):
    for p in range(value.shape[0]):
        for c in range(value.shape[1]):
            ref[plane + p, c, pl.ds(start, value.shape[2], stride=2), :] = value[p, c]


def zero_pads(ref, planes):
    rows = ref.shape[2]
    for plane in planes:
        zero = jnp.zeros((1, ref.shape[1], PAD, LANES), jnp.float32)
        put(ref, plane, 0, zero)
        put(ref, plane, rows - PAD, zero)


def coarse_block(fine, resid, step, fine_row, size):
    def both(ref, plane, count):
        return strided(ref, plane, count, fine_row, size) + strided(
            ref, plane, count, fine_row + 1, size
        )

    f = both(resid, 0, 2)
    kx = strided(fine, KX, 2, fine_row + 1, size)
    ky = both(fine, KY, 2)
    surf_kz = both(fine, S, 3)
    summed = jnp.concatenate([f, kx, surf_kz], axis=0)
    summed = summed + from_right(summed, step)
    return summed[0:2], summed[2:4], from_right(ky, step), summed[4:7]


def sides(mine, other, is_even):
    low = jnp.where(is_even, other, mine)
    high = jnp.where(is_even, mine, other)
    return low, high


def pack_kernel(source, coef_x, coef_y, surface, coef_z, out, sems):
    inputs = ((source, F, 2), (coef_x, KX, 2), (coef_y, KY, 2), (surface, S, 2), (coef_z, KZ, 0))
    copies = []
    for k, (ref, plane, count) in enumerate(inputs):
        to = out.at[plane : plane + count] if count else out.at[plane]
        copies.append(pltpu.make_async_copy(ref, to, sems.at[k]))
    for copy in copies:
        copy.start()
    for copy in copies:
        copy.wait()
    rows, cols = out.shape[1], out.shape[2]
    wall_x = lax.axis_index("gx") == lax.axis_size("gx") - 1
    wall_y = lax.axis_index("gy") == lax.axis_size("gy") - 1
    edge = out[KX : KX + 2, rows - 8 :, :]
    row = lax.broadcasted_iota(jnp.int32, edge.shape, 1)
    out[KX : KX + 2, rows - 8 :, :] = jnp.where(wall_x & (row == 7), 0.0, edge)
    edge = out[KY : KY + 2, :, cols - LANES :]
    out[KY : KY + 2, :, cols - LANES :] = jnp.where(
        wall_y & (lane_iota(edge.shape) == LANES - 1), 0.0, edge
    )


def strip_kernel(own_ref, near_ref, far_ref, c_ref, d_ref):
    even_x = lax.rem(lax.axis_index("gx"), 2) == 0
    even_y = lax.rem(lax.axis_index("gy"), 2) == 0
    rows = own_ref.shape[1]
    cols = own_ref.shape[2]
    lane = lane_iota((8, LANES))

    def place(pieces, offset):
        tiles = [jnp.zeros((8, LANES), jnp.float32)] * 2
        for p in range(PLANES):
            begin = p * WIDTH
            rolled = pltpu.roll(pieces[p], (begin - offset) % LANES, 1)
            for a in range(2):
                lo, hi = begin - a * LANES, begin + WIDTH - a * LANES
                if hi > 0 and lo < LANES:
                    tiles[a] = jnp.where((lane >= lo) & (lane < hi), rolled, tiles[a])
        return tiles

    for block in range(3 * rows // 8):
        part, r0 = divmod(block * 8, rows)
        first, last = [], []
        for p in range(PLANES):
            for held, column in ((first, 0), (last, cols - LANES)):
                at = (p, slice(r0, r0 + 8), slice(column, column + LANES))
                if part == 1:
                    held.append(own_ref[at])
                else:
                    held.append(sides(near_ref[at], far_ref[at], even_x)[part // 2])
        left = place(first, 0)
        right = place(last, LANES - WIDTH)
        for a in range(2):
            at = (slice(block * 8, block * 8 + 8), slice(a * LANES, (a + 1) * LANES))
            c_ref[at] = jnp.where(even_y, right[a], left[a])
            d_ref[at] = jnp.where(even_y, left[a], right[a])


def down_kernel(own_ref, near_ref, far_ref, c_ref, d_ref, l0, l1, l2, pack_ref, ua, rr):
    even_x = lax.rem(lax.axis_index("gx"), 2) == 0
    even_y = lax.rem(lax.axis_index("gy"), 2) == 0
    rows = own_ref.shape[1]
    lane = lane_iota((8, LANES))

    def take(tiles, p, offset):
        begin = p * WIDTH
        a, b = begin // LANES, (begin + WIDTH - 1) // LANES
        piece = tiles[a]
        if a != b:
            piece = jnp.where(lane < begin + WIDTH - b * LANES, tiles[b], tiles[a])
        return pltpu.roll(piece, (offset - begin) % LANES, 1)

    for block in range(3 * rows // 8):
        part, r0 = divmod(block * 8, rows)
        to = slice(PAD + block * 8, PAD + block * 8 + 8)
        for p in range(PLANES):
            for c in range(2):
                at = (p, slice(r0, r0 + 8), slice(c * LANES, (c + 1) * LANES))
                if part == 1:
                    l0[p, c, to, :] = own_ref[at]
                else:
                    l0[p, c, to, :] = sides(near_ref[at], far_ref[at], even_x)[part // 2]
        low, high = [], []
        for a in range(2):
            at = (slice(block * 8, block * 8 + 8), slice(a * LANES, (a + 1) * LANES))
            lo, hi = sides(c_ref[at], d_ref[at], even_y)
            low.append(lo)
            high.append(hi)
        for p in range(PLANES):
            right = take(high, p, 0)
            left = take(low, p, LANES - WIDTH)
            l0[p, 2, to, :] = jnp.where(
                lane < WIDTH, right, jnp.where(lane >= LANES - WIDTH, left, 0.0)
            )

    for ref in (l0, l1, l2):
        zero_pads(ref, (KX, KX + 1, U, U + 1))
    for ref in (ua,):
        zero_pads(ref, (0, 1))

    levels = (l0, l1, l2)
    for depth, level in enumerate(levels):
        step = 1 << depth
        count = level.shape[2] - 2 * PAD
        starts = range(PAD, PAD + count, 8)
        if depth:
            for r0 in starts:
                f, kx, ky, surf_kz = coarse_block(
                    levels[depth - 1], rr, step // 2, PAD + 2 * (r0 - PAD), 8
                )
                put(level, F, r0, f)
                put(level, KX, r0, kx)
                put(level, KY, r0, ky)
                put(level, S, r0, surf_kz)
            if count * 2 + 2 * PAD > 0:
                put(ua, 0, PAD + count, jnp.zeros((2, 3, PAD, LANES), jnp.float32))
        for r0 in starts:
            w = weight(
                rows_of(level, KX, 2, r0),
                rows_of(level, KX, 2, r0 - 1),
                rows_of(level, KY, 2, r0),
                rows_of(level, KZ, 1, r0),
                rows_of(level, S, 2, r0),
                step,
            )
            put(level, W, r0, w)
            put(ua, 0, r0, w * rows_of(level, F, 2, r0))
        for r0 in starts:
            u, r = block_residual(level, ua, 0, step, r0)
            put(level, U, r0, u + rows_of(level, W, 2, r0) * r)
        for r0 in starts:
            put(rr, 0, r0, block_residual(level, level, U, step, r0)[1])

    own = l2.shape[2] // 2 - 4
    f, kx, ky, surf_kz = coarse_block(l2, rr, 4, own, 4)
    nine = jnp.concatenate([f, kx, ky, surf_kz], axis=0)
    total = jnp.zeros((PLANES, LANES), jnp.float32)
    for r in range(4):
        for c in range(2):
            src = lax.broadcasted_iota(jnp.int32, (LANES, LANES), 0) + c * LANES
            dst = lax.broadcasted_iota(jnp.int32, (LANES, LANES), 1) - r * 32
            pick = jnp.where((src == dst * 8) & (dst >= 0) & (dst < 32), 1.0, 0.0)
            total = total + jnp.dot(
                nine[:, c, r, :],
                pick,
                precision=lax.Precision.HIGHEST,
                preferred_element_type=jnp.float32,
            )
    pack_ref[0, 0:PLANES, :] = total
    pack_ref[0, PLANES:PACK, :] = jnp.zeros((PACK - PLANES, LANES), jnp.float32)


def whole_sweep(level, u, weights, step):
    f, kx, kx_lo, ky, kz, surf = level
    rows = u.shape[2]
    r = residual_of(
        f, u, pltpu.roll(u, rows - 1, 2), pltpu.roll(u, 1, 2), kx, kx_lo, ky, kz, surf, step
    )
    return u + weights * r, r


def up_kernel(nx, ny, x_ref, l0, l1, l2, p_ref, r_ref, xs, g3, g4, ub, uc, sem):
    me_x = lax.axis_index("gx")
    me_y = lax.axis_index("gy")
    tiles = ny // 4
    rows3 = nx * 4

    copy = pltpu.make_async_copy(x_ref, xs, sem)
    copy.start()
    copy.wait()

    lane = lane_iota((rows3, LANES))
    row = lax.broadcasted_iota(jnp.int32, (rows3, LANES), 0)
    for p in range(PLANES):
        for q in range(tiles):
            if tiles == 1:
                x = xs[pl.ds(p, rows3, stride=PACK), :]
            else:
                x = jnp.concatenate(
                    [
                        xs[pl.ds((i * ny + 4 * q) * PACK + p, 4, stride=PACK), :]
                        for i in range(nx)
                    ],
                    axis=0,
                )
            out = x
            for delta in range(-3, 4):
                if delta == 0:
                    continue
                moved = pltpu.roll(x, (-delta) % rows3, 0)
                moved = pltpu.roll(moved, (32 * delta) % LANES, 1)
                out = jnp.where(lane // 32 - row % 4 == delta, moved, out)
            g3[p, q, :, :] = out

    def gathered(ref):
        kx = ref[KX : KX + 2]
        return (
            ref[F : F + 2],
            kx,
            pltpu.roll(kx, 1, 2),
            ref[KY : KY + 2],
            ref[KZ : KZ + 1],
            ref[S : S + 2],
        )

    level3 = gathered(g3)
    w3 = weight(*level3[1:], 1)
    u3 = w3 * level3[0]
    u3, unused = whole_sweep(level3, u3, w3, 1)
    unused, r3 = whole_sweep(level3, u3, w3, 1)
    g4[0:2] = r3
    f, kx, ky, surf_kz = coarse_block(g3, g4, 1, 0, rows3 // 2)
    level4 = (f, kx, pltpu.roll(kx, 1, 2), ky, surf_kz[2:3], surf_kz[0:2])
    w4 = weight(*level4[1:], 2)
    u4 = w4 * f
    for step in range(CSWEEPS - 1):
        u4, unused = whole_sweep(level4, u4, w4, 2)
    unused, rc = whole_sweep(level4, u4, w4, 2)
    even = lane_iota(u4.shape) % 2 == 0

    def total(x):
        x = jnp.sum(jnp.where(even, x, 0.0), axis=(0, 1))
        return jnp.sum(jnp.sum(x, axis=0, keepdims=True), axis=1, keepdims=True)

    e4 = u4 + (total(rc) / total(level4[5]))[None, None]
    e4 = jnp.where(even, e4, from_left(e4, 1))
    put_strided(g4, 0, 0, e4)
    put_strided(g4, 0, 1, e4)
    u3 = u3 + g4[0:2]
    for step in range(POST):
        u3, unused = whole_sweep(level3, u3, w3, 1)

    rows2 = l2.shape[2] - 2 * PAD
    to_row = lax.broadcasted_iota(jnp.int32, (rows2, rows3), 0) // 2 - 4 + me_x * 4
    pick_row = jnp.where(
        to_row == lax.broadcasted_iota(jnp.int32, (rows2, rows3), 1), 1.0, 0.0
    )
    dot = functools.partial(
        jnp.dot, precision=lax.Precision.HIGHEST, preferred_element_type=jnp.float32
    )
    near = [[dot(pick_row, u3[k, q]) for q in range(tiles)] for k in range(2)]
    near = [jnp.concatenate([near[k][q] for k in range(2)], axis=0) for q in range(tiles)]
    for c in range(3):
        spread = jnp.zeros((2 * rows2, LANES), jnp.float32)
        for q in range(tiles):
            column = lax.broadcasted_iota(jnp.int32, (LANES, LANES), 1) + c * LANES
            column = jnp.where(column >= 320, column - 384, column)
            coarse = (column + 64) // 8 - 8 + me_y * 32 - q * LANES
            pick = jnp.where(
                coarse == lax.broadcasted_iota(jnp.int32, (LANES, LANES), 0), 1.0, 0.0
            )
            spread = spread + dot(near[q], pick)
        for k in range(2):
            uc[k, c, PAD : PAD + rows2, :] = spread[k * rows2 : (k + 1) * rows2]

    levels = (l0, l1, l2)
    zeros = jnp.zeros((2, 3, PAD, LANES), jnp.float32)
    for depth in (2, 1, 0):
        level = levels[depth]
        step = 1 << depth
        count = level.shape[2] - 2 * PAD
        margin = (24, 8, 0)[depth]
        starts = range(PAD + margin, PAD + count - margin, 8)
        for r0 in starts:
            put(uc, 0, r0, rows_of(uc, 0, 2, r0) + rows_of(level, U, 2, r0))
        for buf in (uc, ub):
            put(buf, 0, PAD + margin - 8, zeros)
            put(buf, 0, PAD + count - margin, zeros)
        for source, target in ((uc, ub), (ub, uc)):
            for r0 in starts:
                u, r = block_residual(level, source, 0, step, r0)
                put(target, 0, r0, u + rows_of(level, W, 2, r0) * r)
        if depth:
            finer = levels[depth - 1]
            need = (24, 8, 0)[depth - 1]
            half = step // 2
            first, last = need // 2, (finer.shape[2] - 2 * PAD - need) // 2
            blocks = []
            for r0 in range(first, last, 4):
                e = rows_of(uc, 0, 2, PAD + r0, 4)
                blocks.append(
                    jnp.where(lane_iota(e.shape) % step < half, e, from_left(e, half))
                )
            for r0, e in zip(range(first, last, 4), blocks):
                put_strided(ub, 0, PAD + 2 * r0, e)
                put_strided(ub, 0, PAD + 2 * r0 + 1, e)
            for r0 in range(PAD + need, PAD + 2 * last, 8):
                put(uc, 0, r0, rows_of(ub, 0, 2, r0))
        else:
            own = p_ref.shape[1]
            for r0 in range(0, own, 8):
                at = PAD + count // 2 - own // 2 + r0
                u, r = block_residual(level, uc, 0, step, at)
                for c in range(2):
                    p_ref[:, r0 : r0 + 8, c * LANES : (c + 1) * LANES] = u[:, c]
                    r_ref[:, r0 : r0 + 8, c * LANES : (c + 1) * LANES] = r[:, c]


def shape_of(*shape):
    return jax.ShapeDtypeStruct(shape, jnp.float32)


def vmem(*shape):
    return pltpu.VMEM(shape, jnp.float32)


def on_device(source, coef_x, coef_y, coef_z, surface):
    rows, cols = source.shape[1], source.shape[2]
    nx, ny = lax.axis_size("gx"), lax.axis_size("gy")
    params = pltpu.CompilerParams(vmem_limit_bytes=24 * 1024 * 1024)
    packed = pl.pallas_call(
        pack_kernel,
        out_shape=shape_of(PLANES, rows, cols),
        in_specs=[pl.BlockSpec(memory_space=pltpu.HBM)] * 5,
        scratch_shapes=[pltpu.SemaphoreType.DMA((5,))],
        compiler_params=params,
        name="pack",
    )(
        *(
            pltpu.with_memory_space_constraint(x, pltpu.HBM)
            for x in (source, coef_x, coef_y, surface, coef_z)
        )
    )

    near = pair_permute(packed, "gx", 0)
    far = pair_permute(packed, "gx", 1)
    strips = pl.pallas_call(
        strip_kernel,
        out_shape=(shape_of(3 * rows, 2 * LANES),) * 2,
        compiler_params=params,
        name="strips",
    )(packed, near, far)
    strip_c = pair_permute(strips[0], "gy", 0)
    strip_d = pair_permute(strips[1], "gy", 1)

    heights = [3 * rows // (1 << depth) + 2 * PAD for depth in range(3)]
    planes = U + 2
    l0, l1, l2, pack = pl.pallas_call(
        down_kernel,
        out_shape=tuple(shape_of(planes, 3, h, LANES) for h in heights)
        + (shape_of(1, PACK, LANES),),
        scratch_shapes=[vmem(2, 3, heights[0], LANES)] * 2,
        compiler_params=params,
        name="down",
    )(packed, near, far, strip_c, strip_d)

    everyone = lax.all_to_all(
        jnp.broadcast_to(pack, (nx * ny, PACK, LANES)), ("gx", "gy"), 0, 0, tiled=True
    ).reshape(nx * ny * PACK, LANES)

    tiles = ny // 4
    pressure, residual = pl.pallas_call(
        functools.partial(up_kernel, nx, ny),
        out_shape=(shape_of(*source.shape),) * 2,
        scratch_shapes=[
            vmem(nx * ny * PACK, LANES),
            vmem(PLANES, tiles, nx * 4, LANES),
            vmem(2, tiles, nx * 4, LANES),
            vmem(2, 3, heights[0], LANES),
            vmem(2, 3, heights[0], LANES),
            pltpu.SemaphoreType.DMA,
        ],
        in_specs=[pl.BlockSpec(memory_space=pltpu.HBM)]
        + [pl.BlockSpec(memory_space=pltpu.VMEM)] * 3,
        compiler_params=params,
        name="up",
    )(pltpu.with_memory_space_constraint(everyone, pltpu.HBM), l0, l1, l2)
    return pressure, residual


def solution(mesh):
    layered, plane = P(None, "gx", "gy"), P("gx", "gy")
    return jax.shard_map(
        on_device,
        mesh=mesh,
        in_specs=(layered, layered, layered, plane, layered),
        out_specs=(layered, layered),
        check_vma=False,
    )
```

```python
import functools

import jax
import jax.numpy as jnp
from jax import lax
from jax.experimental import pallas as pl
from jax.experimental.pallas import tpu as pltpu
from jax.sharding import PartitionSpec as P

LEVELS = 4
PRE = 2
POST = 2
CSWEEPS = 8
damping = 0.8

LANES = 128
WIDTH = 28
PAD = 8
PLANES = 9
PACK = PLANES * LANES
F, KX, KY, S, KZ = 0, 2, 4, 6, 8
W, U = 9, 11


def pair_permute(x, axis, first, wrap=False):
    count = lax.axis_size(axis)
    pairs = []
    for i in range(first, count if wrap else count - 1, 2):
        pairs += [(i, (i + 1) % count), ((i + 1) % count, i)]
    return lax.ppermute(x, axis, pairs)


def far_permute(x):
    nx, ny = lax.axis_size("gx"), lax.axis_size("gy")
    pairs = []
    for i in range(nx):
        for j in range(ny):
            to = (i, j ^ 2) if i in (0, nx - 1) else (((i - 1) ^ 1) + 1, j)
            pairs.append((i * ny + j, to[0] * ny + to[1]))
    return lax.ppermute(x, ("gx", "gy"), pairs)


def lane_iota(shape):
    return lax.broadcasted_iota(jnp.int32, shape, len(shape) - 1)


def from_right(x, step):
    rolled = pltpu.roll(x, LANES - step, x.ndim - 1)
    if x.shape[1] == 1:
        return rolled
    after = jnp.concatenate([rolled[:, 1:], rolled[:, :1]], axis=1)
    return jnp.where(lane_iota(x.shape) >= LANES - step, after, rolled)


def from_left(x, step):
    rolled = pltpu.roll(x, step, x.ndim - 1)
    if x.shape[1] == 1:
        return rolled
    before = jnp.concatenate([rolled[:, -1:], rolled[:, :-1]], axis=1)
    return jnp.where(lane_iota(x.shape) < step, before, rolled)


def weight(kx, kx_lo, ky, kz, surf, step):
    diag = surf + kx + kx_lo + ky + from_left(ky, step) + kz
    return jnp.where(diag > 0.0, damping / jnp.where(diag > 0.0, diag, 1.0), 0.0)


def residual_of(f, u, u_up, u_dn, kx, kx_lo, ky, kz, surf, step):
    flux = ky * (u - from_right(u, step))
    vert = kz * (u[0:1] - u[1:2])
    out = surf * u + kx * (u - u_up) + kx_lo * (u - u_dn)
    out = out + flux - from_left(flux, step)
    return f - (out + jnp.concatenate([vert, -vert], axis=0))


def rows_of(ref, plane, count, start, size=8):
    return ref[plane : plane + count, :, start : start + size, :]


def block_residual(level, u_ref, u_at, step, r0):
    u = rows_of(u_ref, u_at, 2, r0)
    return u, residual_of(
        rows_of(level, F, 2, r0),
        u,
        rows_of(u_ref, u_at, 2, r0 + 1),
        rows_of(u_ref, u_at, 2, r0 - 1),
        rows_of(level, KX, 2, r0),
        rows_of(level, KX, 2, r0 - 1),
        rows_of(level, KY, 2, r0),
        rows_of(level, KZ, 1, r0),
        rows_of(level, S, 2, r0),
        step,
    )


def put(ref, plane, r0, value):
    ref[plane : plane + value.shape[0], :, r0 : r0 + value.shape[2], :] = value


def strided(ref, plane, count, start, size):
    tiles = ref.shape[1]
    return jnp.stack(
        [
            jnp.stack([ref[plane + p, c, pl.ds(start, size, stride=2), :] for c in range(tiles)])
            for p in range(count)
        ]
    )


def put_strided(ref, plane, start, value):
    for p in range(value.shape[0]):
        for c in range(value.shape[1]):
            ref[plane + p, c, pl.ds(start, value.shape[2], stride=2), :] = value[p, c]


def zero_pads(ref, planes):
    rows = ref.shape[2]
    for plane in planes:
        zero = jnp.zeros((1, ref.shape[1], PAD, LANES), jnp.float32)
        put(ref, plane, 0, zero)
        put(ref, plane, rows - PAD, zero)


def coarse_block(fine, resid, step, fine_row, size):
    def both(ref, plane, count):
        return strided(ref, plane, count, fine_row, size) + strided(
            ref, plane, count, fine_row + 1, size
        )

    f = both(resid, 0, 2)
    kx = strided(fine, KX, 2, fine_row + 1, size)
    ky = both(fine, KY, 2)
    surf_kz = both(fine, S, 3)
    summed = jnp.concatenate([f, kx, surf_kz], axis=0)
    summed = summed + from_right(summed, step)
    return summed[0:2], summed[2:4], from_right(ky, step), summed[4:7]


def sides(mine, other, is_even):
    low = jnp.where(is_even, other, mine)
    high = jnp.where(is_even, mine, other)
    return low, high


def sides_x(near, far):
    me = lax.axis_index("gx")
    low, high = sides(near, far, lax.rem(me, 2) == 0)
    return jnp.where(me == 0, 0.0, low), high


def pack_kernel(source, coef_x, coef_y, surface, coef_z, out, c_ref, d_ref, sems):
    inputs = ((source, F, 2), (coef_x, KX, 2), (coef_y, KY, 2), (surface, S, 2), (coef_z, KZ, 0))
    copies = []
    for k, (ref, plane, count) in enumerate(inputs):
        to = out.at[plane : plane + count] if count else out.at[plane]
        copies.append(pltpu.make_async_copy(ref, to, sems.at[k]))
    for copy in copies:
        copy.start()
    for copy in copies:
        copy.wait()
    rows, cols = out.shape[1], out.shape[2]
    wall_x = lax.axis_index("gx") == lax.axis_size("gx") - 1
    wall_y = lax.axis_index("gy") == lax.axis_size("gy") - 1
    edge = out[KX : KX + 2, rows - 8 :, :]
    row = lax.broadcasted_iota(jnp.int32, edge.shape, 1)
    out[KX : KX + 2, rows - 8 :, :] = jnp.where(wall_x & (row == 7), 0.0, edge)
    edge = out[KY : KY + 2, :, cols - LANES :]
    out[KY : KY + 2, :, cols - LANES :] = jnp.where(
        wall_y & (lane_iota(edge.shape) == LANES - 1), 0.0, edge
    )

    even_y = lax.rem(lax.axis_index("gy"), 2) == 0
    lane = lane_iota((8, LANES))
    for r0 in range(0, rows, 8):
        left = [jnp.zeros((8, LANES), jnp.float32)] * 2
        right = list(left)
        for p in range(PLANES):
            begin = p * WIDTH
            for tiles, column, offset in ((left, 0, 0), (right, cols - LANES, LANES - WIDTH)):
                piece = out[p, r0 : r0 + 8, column : column + LANES]
                rolled = pltpu.roll(piece, (begin - offset) % LANES, 1)
                for a in range(2):
                    lo, hi = begin - a * LANES, begin + WIDTH - a * LANES
                    if hi > 0 and lo < LANES:
                        tiles[a] = jnp.where((lane >= lo) & (lane < hi), rolled, tiles[a])
        for a in range(2):
            at = (slice(r0, r0 + 8), slice(a * LANES, (a + 1) * LANES))
            c_ref[at] = jnp.where(even_y, right[a], left[a])
            d_ref[at] = jnp.where(even_y, left[a], right[a])


def down_kernel(
    own_ref, near_ref, far_ref, own_cd, near_cd, far_cd, l0, l1, l2, pack_ref, ua, rr
):
    even_y = lax.rem(lax.axis_index("gy"), 2) == 0
    rows = own_ref.shape[1]
    lane = lane_iota((8, LANES))

    def take(tiles, p, offset):
        begin = p * WIDTH
        a, b = begin // LANES, (begin + WIDTH - 1) // LANES
        piece = tiles[a]
        if a != b:
            piece = jnp.where(lane < begin + WIDTH - b * LANES, tiles[b], tiles[a])
        return pltpu.roll(piece, (offset - begin) % LANES, 1)

    for block in range(3 * rows // 8):
        part, r0 = divmod(block * 8, rows)
        to = slice(PAD + block * 8, PAD + block * 8 + 8)
        for p in range(PLANES):
            for c in range(2):
                at = (p, slice(r0, r0 + 8), slice(c * LANES, (c + 1) * LANES))
                if part == 1:
                    l0[p, c, to, :] = own_ref[at]
                else:
                    l0[p, c, to, :] = sides_x(near_ref[at], far_ref[at])[part // 2]
        low, high = [], []
        for a in range(2):
            held = []
            for base in (0, rows):
                at = (slice(base + r0, base + r0 + 8), slice(a * LANES, (a + 1) * LANES))
                if part == 1:
                    held.append(own_cd[at])
                else:
                    held.append(sides_x(near_cd[at], far_cd[at])[part // 2])
            lo, hi = sides(held[0], held[1], even_y)
            low.append(lo)
            high.append(hi)
        for p in range(PLANES):
            right = take(high, p, 0)
            left = take(low, p, LANES - WIDTH)
            l0[p, 2, to, :] = jnp.where(
                lane < WIDTH, right, jnp.where(lane >= LANES - WIDTH, left, 0.0)
            )

    for ref in (l0, l1, l2):
        zero_pads(ref, (KX, KX + 1, U, U + 1))
    for ref in (ua,):
        zero_pads(ref, (0, 1))

    levels = (l0, l1, l2)
    for depth, level in enumerate(levels):
        step = 1 << depth
        count = level.shape[2] - 2 * PAD
        starts = range(PAD, PAD + count, 8)
        if depth:
            for r0 in starts:
                f, kx, ky, surf_kz = coarse_block(
                    levels[depth - 1], rr, step // 2, PAD + 2 * (r0 - PAD), 8
                )
                put(level, F, r0, f)
                put(level, KX, r0, kx)
                put(level, KY, r0, ky)
                put(level, S, r0, surf_kz)
            if count * 2 + 2 * PAD > 0:
                put(ua, 0, PAD + count, jnp.zeros((2, 3, PAD, LANES), jnp.float32))
        for r0 in starts:
            w = weight(
                rows_of(level, KX, 2, r0),
                rows_of(level, KX, 2, r0 - 1),
                rows_of(level, KY, 2, r0),
                rows_of(level, KZ, 1, r0),
                rows_of(level, S, 2, r0),
                step,
            )
            put(level, W, r0, w)
            put(ua, 0, r0, w * rows_of(level, F, 2, r0))
        for r0 in starts:
            u, r = block_residual(level, ua, 0, step, r0)
            put(level, U, r0, u + rows_of(level, W, 2, r0) * r)
        for r0 in starts:
            put(rr, 0, r0, block_residual(level, level, U, step, r0)[1])

    own = l2.shape[2] // 2 - 4
    f, kx, ky, surf_kz = coarse_block(l2, rr, 4, own, 4)
    nine = jnp.concatenate([f, kx, ky, surf_kz], axis=0)
    total = jnp.zeros((PLANES, LANES), jnp.float32)
    for r in range(4):
        for c in range(2):
            src = lax.broadcasted_iota(jnp.int32, (LANES, LANES), 0) + c * LANES
            dst = lax.broadcasted_iota(jnp.int32, (LANES, LANES), 1) - r * 32
            pick = jnp.where((src == dst * 8) & (dst >= 0) & (dst < 32), 1.0, 0.0)
            total = total + jnp.dot(
                nine[:, c, r, :],
                pick,
                precision=lax.Precision.HIGHEST,
                preferred_element_type=jnp.float32,
            )
    for p in range(PLANES):
        at = slice(p * LANES, (p + 1) * LANES)
        pack_ref[:, :, at] = jnp.broadcast_to(
            total[p : p + 1][None], (pack_ref.shape[0], 1, LANES)
        )


def whole_sweep(level, u, weights, step):
    f, kx, kx_lo, ky, kz, surf = level
    rows = u.shape[2]
    r = residual_of(
        f, u, pltpu.roll(u, rows - 1, 2), pltpu.roll(u, 1, 2), kx, kx_lo, ky, kz, surf, step
    )
    return u + weights * r, r


def up_kernel(nx, ny, x_ref, l0, l1, l2, p_ref, r_ref, g3, g4, ub, uc):
    me_x = lax.axis_index("gx")
    me_y = lax.axis_index("gy")
    tiles = ny // 4
    rows3 = nx * 4

    lane = lane_iota((rows3, LANES))
    row = lax.broadcasted_iota(jnp.int32, (rows3, LANES), 0)
    for p in range(PLANES):
        for q in range(tiles):
            if tiles == 1:
                x = x_ref[pl.ds(p, rows3, stride=PLANES), :]
            else:
                x = jnp.concatenate(
                    [
                        x_ref[pl.ds((i * ny + 4 * q) * PLANES + p, 4, stride=PLANES), :]
                        for i in range(nx)
                    ],
                    axis=0,
                )
            out = x
            for delta in range(-3, 4):
                if delta == 0:
                    continue
                moved = pltpu.roll(x, (-delta) % rows3, 0)
                moved = pltpu.roll(moved, (32 * delta) % LANES, 1)
                out = jnp.where(lane // 32 - row % 4 == delta, moved, out)
            g3[p, q, :, :] = out

    def gathered(ref):
        kx = ref[KX : KX + 2]
        return (
            ref[F : F + 2],
            kx,
            pltpu.roll(kx, 1, 2),
            ref[KY : KY + 2],
            ref[KZ : KZ + 1],
            ref[S : S + 2],
        )

    level3 = gathered(g3)
    w3 = weight(*level3[1:], 1)
    u3 = w3 * level3[0]
    u3, unused = whole_sweep(level3, u3, w3, 1)
    unused, r3 = whole_sweep(level3, u3, w3, 1)
    g4[0:2] = r3
    f, kx, ky, surf_kz = coarse_block(g3, g4, 1, 0, rows3 // 2)
    level4 = (f, kx, pltpu.roll(kx, 1, 2), ky, surf_kz[2:3], surf_kz[0:2])
    w4 = weight(*level4[1:], 2)
    u4 = w4 * f
    for step in range(CSWEEPS - 1):
        u4, unused = whole_sweep(level4, u4, w4, 2)
    unused, rc = whole_sweep(level4, u4, w4, 2)
    even = lane_iota(u4.shape) % 2 == 0

    def total(x):
        x = jnp.sum(jnp.where(even, x, 0.0), axis=(0, 1))
        return jnp.sum(jnp.sum(x, axis=0, keepdims=True), axis=1, keepdims=True)

    e4 = u4 + (total(rc) / total(level4[5]))[None, None]
    e4 = jnp.where(even, e4, from_left(e4, 1))
    put_strided(g4, 0, 0, e4)
    put_strided(g4, 0, 1, e4)
    u3 = u3 + g4[0:2]
    for step in range(POST):
        u3, unused = whole_sweep(level3, u3, w3, 1)

    rows2 = l2.shape[2] - 2 * PAD
    to_row = lax.broadcasted_iota(jnp.int32, (rows2, rows3), 0) // 2 - 4 + me_x * 4
    pick_row = jnp.where(
        to_row == lax.broadcasted_iota(jnp.int32, (rows2, rows3), 1), 1.0, 0.0
    )
    dot = functools.partial(
        jnp.dot, precision=lax.Precision.HIGHEST, preferred_element_type=jnp.float32
    )
    near = [[dot(pick_row, u3[k, q]) for q in range(tiles)] for k in range(2)]
    near = [jnp.concatenate([near[k][q] for k in range(2)], axis=0) for q in range(tiles)]
    for c in range(3):
        spread = jnp.zeros((2 * rows2, LANES), jnp.float32)
        for q in range(tiles):
            column = lax.broadcasted_iota(jnp.int32, (LANES, LANES), 1) + c * LANES
            column = jnp.where(column >= 320, column - 384, column)
            coarse = (column + 64) // 8 - 8 + me_y * 32 - q * LANES
            pick = jnp.where(
                coarse == lax.broadcasted_iota(jnp.int32, (LANES, LANES), 0), 1.0, 0.0
            )
            spread = spread + dot(near[q], pick)
        for k in range(2):
            uc[k, c, PAD : PAD + rows2, :] = spread[k * rows2 : (k + 1) * rows2]

    levels = (l0, l1, l2)
    zeros = jnp.zeros((2, 3, PAD, LANES), jnp.float32)
    for depth in (2, 1, 0):
        level = levels[depth]
        step = 1 << depth
        count = level.shape[2] - 2 * PAD
        margin = (24, 8, 0)[depth]
        starts = range(PAD + margin, PAD + count - margin, 8)
        for r0 in starts:
            put(uc, 0, r0, rows_of(uc, 0, 2, r0) + rows_of(level, U, 2, r0))
        for buf in (uc, ub):
            put(buf, 0, PAD + margin - 8, zeros)
            put(buf, 0, PAD + count - margin, zeros)
        for source, target in ((uc, ub), (ub, uc)):
            for r0 in starts:
                u, r = block_residual(level, source, 0, step, r0)
                put(target, 0, r0, u + rows_of(level, W, 2, r0) * r)
        if depth:
            finer = levels[depth - 1]
            need = (24, 8, 0)[depth - 1]
            half = step // 2
            first, last = need // 2, (finer.shape[2] - 2 * PAD - need) // 2
            blocks = []
            for r0 in range(first, last, 4):
                e = rows_of(uc, 0, 2, PAD + r0, 4)
                blocks.append(
                    jnp.where(lane_iota(e.shape) % step < half, e, from_left(e, half))
                )
            for r0, e in zip(range(first, last, 4), blocks):
                put_strided(ub, 0, PAD + 2 * r0, e)
                put_strided(ub, 0, PAD + 2 * r0 + 1, e)
            for r0 in range(PAD + need, PAD + 2 * last, 8):
                put(uc, 0, r0, rows_of(ub, 0, 2, r0))
        else:
            own = p_ref.shape[1]
            for r0 in range(0, own, 8):
                at = PAD + count // 2 - own // 2 + r0
                u, r = block_residual(level, uc, 0, step, at)
                for c in range(2):
                    p_ref[:, r0 : r0 + 8, c * LANES : (c + 1) * LANES] = u[:, c]
                    r_ref[:, r0 : r0 + 8, c * LANES : (c + 1) * LANES] = r[:, c]


def shape_of(*shape):
    return jax.ShapeDtypeStruct(shape, jnp.float32)


def vmem(*shape):
    return pltpu.VMEM(shape, jnp.float32)


def on_device(source, coef_x, coef_y, coef_z, surface):
    rows, cols = source.shape[1], source.shape[2]
    nx, ny = lax.axis_size("gx"), lax.axis_size("gy")
    params = pltpu.CompilerParams(vmem_limit_bytes=24 * 1024 * 1024)
    packed, strip_c, strip_d = pl.pallas_call(
        pack_kernel,
        out_shape=(shape_of(PLANES, rows, cols),) + (shape_of(rows, 2 * LANES),) * 2,
        in_specs=[pl.BlockSpec(memory_space=pltpu.HBM)] * 5,
        scratch_shapes=[pltpu.SemaphoreType.DMA((5,))],
        compiler_params=params,
        name="pack",
    )(
        *(
            pltpu.with_memory_space_constraint(x, pltpu.HBM)
            for x in (source, coef_x, coef_y, surface, coef_z)
        )
    )

    strip_c = pair_permute(strip_c, "gy", 0)
    strip_d = pair_permute(strip_d, "gy", 1, wrap=True)
    far = far_permute(packed)
    near = pair_permute(packed, "gx", 0)
    strips = jnp.concatenate([strip_c, strip_d], axis=0)
    far_strips = far_permute(strips)
    near_strips = pair_permute(strips, "gx", 0)

    heights = [3 * rows // (1 << depth) + 2 * PAD for depth in range(3)]
    planes = U + 2
    l0, l1, l2, pack = pl.pallas_call(
        down_kernel,
        out_shape=tuple(shape_of(planes, 3, h, LANES) for h in heights)
        + (shape_of(nx * ny, 1, PACK),),
        scratch_shapes=[vmem(2, 3, heights[0], LANES)] * 2,
        compiler_params=params,
        name="down",
    )(packed, near, far, strips, near_strips, far_strips)

    everyone = lax.all_to_all(pack, ("gx", "gy"), 0, 0, tiled=True)
    everyone = everyone.reshape(nx * ny * PLANES, LANES)

    tiles = ny // 4
    pressure, residual = pl.pallas_call(
        functools.partial(up_kernel, nx, ny),
        out_shape=(shape_of(*source.shape),) * 2,
        scratch_shapes=[
            vmem(PLANES, tiles, nx * 4, LANES),
            vmem(2, tiles, nx * 4, LANES),
            vmem(2, 3, heights[0], LANES),
            vmem(2, 3, heights[0], LANES),
        ],
        compiler_params=params,
        name="up",
    )(everyone, l0, l1, l2)
    return pressure, residual


def solution(mesh):
    layered, plane = P(None, "gx", "gy"), P("gx", "gy")
    return jax.shard_map(
        on_device,
        mesh=mesh,
        in_specs=(layered, layered, layered, plane, layered),
        out_specs=(layered, layered),
        check_vma=False,
    )
```

```python
import functools

import jax
import jax.numpy as jnp
from jax import lax
from jax.experimental import pallas as pl
from jax.experimental.pallas import tpu as pltpu
from jax.sharding import PartitionSpec as P

LEVELS = 4
PRE = 2
POST = 2
CSWEEPS = 8
damping = 0.8

LANES = 128
WIDTH = 28
PAD = 8
PLANES = 9
PACK = PLANES * LANES
F, KX, KY, S, KZ = 0, 2, 4, 6, 8
W, U = 9, 11


def pair_permute(x, axis, first, wrap=False):
    count = lax.axis_size(axis)
    pairs = []
    for i in range(first, count if wrap else count - 1, 2):
        pairs += [(i, (i + 1) % count), ((i + 1) % count, i)]
    return lax.ppermute(x, axis, pairs)


def far_permute(x):
    nx, ny = lax.axis_size("gx"), lax.axis_size("gy")
    pairs = []
    for i in range(nx):
        for j in range(ny):
            to = (i, j ^ 2) if i in (0, nx - 1) else (((i - 1) ^ 1) + 1, j)
            pairs.append((i * ny + j, to[0] * ny + to[1]))
    return lax.ppermute(x, ("gx", "gy"), pairs)


def lane_iota(shape):
    return lax.broadcasted_iota(jnp.int32, shape, len(shape) - 1)


def from_right(x, step):
    rolled = pltpu.roll(x, LANES - step, x.ndim - 1)
    if x.shape[1] == 1:
        return rolled
    after = jnp.concatenate([rolled[:, 1:], rolled[:, :1]], axis=1)
    return jnp.where(lane_iota(x.shape) >= LANES - step, after, rolled)


def from_left(x, step):
    rolled = pltpu.roll(x, step, x.ndim - 1)
    if x.shape[1] == 1:
        return rolled
    before = jnp.concatenate([rolled[:, -1:], rolled[:, :-1]], axis=1)
    return jnp.where(lane_iota(x.shape) < step, before, rolled)


def weight(kx, kx_lo, ky, kz, surf, step):
    diag = surf + kx + kx_lo + ky + from_left(ky, step) + kz
    return jnp.where(diag > 0.0, damping / jnp.where(diag > 0.0, diag, 1.0), 0.0)


def residual_of(f, u, u_up, u_dn, kx, kx_lo, ky, kz, surf, step):
    flux = ky * (u - from_right(u, step))
    vert = kz * (u[0:1] - u[1:2])
    out = surf * u + kx * (u - u_up) + kx_lo * (u - u_dn)
    out = out + flux - from_left(flux, step)
    return f - (out + jnp.concatenate([vert, -vert], axis=0))


def lane_take(x, index):
    parts = [
        jnp.take_along_axis(x[r : r + 8], index[r : r + 8], axis=1, mode="promise_in_bounds")
        for r in range(0, x.shape[0], 8)
    ]
    return parts[0] if len(parts) == 1 else jnp.concatenate(parts, axis=0)


def row_take(x, index):
    parts = [
        jnp.take_along_axis(x[r : r + 8], index[r : r + 8], axis=0, mode="promise_in_bounds")
        for r in range(0, x.shape[0], 8)
    ]
    return parts[0] if len(parts) == 1 else jnp.concatenate(parts, axis=0)


def rows_of(ref, plane, count, start, size=8):
    return ref[plane : plane + count, :, start : start + size, :]


def block_residual(level, u_ref, u_at, step, r0):
    u = rows_of(u_ref, u_at, 2, r0)
    return u, residual_of(
        rows_of(level, F, 2, r0),
        u,
        rows_of(u_ref, u_at, 2, r0 + 1),
        rows_of(u_ref, u_at, 2, r0 - 1),
        rows_of(level, KX, 2, r0),
        rows_of(level, KX, 2, r0 - 1),
        rows_of(level, KY, 2, r0),
        rows_of(level, KZ, 1, r0),
        rows_of(level, S, 2, r0),
        step,
    )


def put(ref, plane, r0, value):
    ref[plane : plane + value.shape[0], :, r0 : r0 + value.shape[2], :] = value


def strided(ref, plane, count, start, size):
    tiles = ref.shape[1]
    return jnp.stack(
        [
            jnp.stack([ref[plane + p, c, pl.ds(start, size, stride=2), :] for c in range(tiles)])
            for p in range(count)
        ]
    )


def put_strided(ref, plane, start, value):
    for p in range(value.shape[0]):
        for c in range(value.shape[1]):
            ref[plane + p, c, pl.ds(start, value.shape[2], stride=2), :] = value[p, c]


def zero_pads(ref, planes):
    rows = ref.shape[2]
    for plane in planes:
        zero = jnp.zeros((1, ref.shape[1], PAD, LANES), jnp.float32)
        put(ref, plane, 0, zero)
        put(ref, plane, rows - PAD, zero)


def coarse_block(fine, resid, step, fine_row, size):
    def both(ref, plane, count):
        return strided(ref, plane, count, fine_row, size) + strided(
            ref, plane, count, fine_row + 1, size
        )

    f = both(resid, 0, 2)
    kx = strided(fine, KX, 2, fine_row + 1, size)
    ky = both(fine, KY, 2)
    surf_kz = both(fine, S, 3)
    summed = jnp.concatenate([f, kx, surf_kz], axis=0)
    summed = summed + from_right(summed, step)
    return summed[0:2], summed[2:4], from_right(ky, step), summed[4:7]


def sides(mine, other, is_even):
    low = jnp.where(is_even, other, mine)
    high = jnp.where(is_even, mine, other)
    return low, high


def sides_x(near, far):
    me = lax.axis_index("gx")
    low, high = sides(near, far, lax.rem(me, 2) == 0)
    return jnp.where(me == 0, 0.0, low), high


def pack_kernel(source, coef_x, coef_y, surface, coef_z, out, c_ref, d_ref, sems):
    inputs = ((source, F, 2), (coef_x, KX, 2), (coef_y, KY, 2), (surface, S, 2), (coef_z, KZ, 0))
    copies = []
    for k, (ref, plane, count) in enumerate(inputs):
        to = out.at[plane : plane + count] if count else out.at[plane]
        copies.append(pltpu.make_async_copy(ref, to, sems.at[k]))
    for copy in copies:
        copy.start()
    for copy in copies:
        copy.wait()
    rows, cols = out.shape[1], out.shape[2]
    wall_x = lax.axis_index("gx") == lax.axis_size("gx") - 1
    wall_y = lax.axis_index("gy") == lax.axis_size("gy") - 1
    edge = out[KX : KX + 2, rows - 8 :, :]
    row = lax.broadcasted_iota(jnp.int32, edge.shape, 1)
    out[KX : KX + 2, rows - 8 :, :] = jnp.where(wall_x & (row == 7), 0.0, edge)
    edge = out[KY : KY + 2, :, cols - LANES :]
    out[KY : KY + 2, :, cols - LANES :] = jnp.where(
        wall_y & (lane_iota(edge.shape) == LANES - 1), 0.0, edge
    )

    even_y = lax.rem(lax.axis_index("gy"), 2) == 0
    lane = lane_iota((8, LANES))
    for r0 in range(0, rows, 8):
        left = [jnp.zeros((8, LANES), jnp.float32)] * 2
        right = list(left)
        for p in range(PLANES):
            begin = p * WIDTH
            for tiles, column, offset in ((left, 0, 0), (right, cols - LANES, LANES - WIDTH)):
                piece = out[p, r0 : r0 + 8, column : column + LANES]
                rolled = pltpu.roll(piece, (begin - offset) % LANES, 1)
                for a in range(2):
                    lo, hi = begin - a * LANES, begin + WIDTH - a * LANES
                    if hi > 0 and lo < LANES:
                        tiles[a] = jnp.where((lane >= lo) & (lane < hi), rolled, tiles[a])
        for a in range(2):
            at = (slice(r0, r0 + 8), slice(a * LANES, (a + 1) * LANES))
            c_ref[at] = jnp.where(even_y, right[a], left[a])
            d_ref[at] = jnp.where(even_y, left[a], right[a])


def down_kernel(
    own_ref, near_ref, far_ref, own_cd, near_cd, far_cd, l0, l1, l2, pack_ref, ua, rr
):
    even_y = lax.rem(lax.axis_index("gy"), 2) == 0
    rows = own_ref.shape[1]
    lane = lane_iota((8, LANES))

    def take(tiles, p, offset):
        begin = p * WIDTH
        a, b = begin // LANES, (begin + WIDTH - 1) // LANES
        piece = tiles[a]
        if a != b:
            piece = jnp.where(lane < begin + WIDTH - b * LANES, tiles[b], tiles[a])
        return pltpu.roll(piece, (offset - begin) % LANES, 1)

    for block in range(3 * rows // 8):
        part, r0 = divmod(block * 8, rows)
        to = slice(PAD + block * 8, PAD + block * 8 + 8)
        for p in range(PLANES):
            for c in range(2):
                at = (p, slice(r0, r0 + 8), slice(c * LANES, (c + 1) * LANES))
                if part == 1:
                    l0[p, c, to, :] = own_ref[at]
                else:
                    l0[p, c, to, :] = sides_x(near_ref[at], far_ref[at])[part // 2]
        low, high = [], []
        for a in range(2):
            held = []
            for base in (rows, 0):
                at = (slice(base + r0, base + r0 + 8), slice(a * LANES, (a + 1) * LANES))
                if part == 1:
                    held.append(own_cd[at])
                else:
                    held.append(sides_x(near_cd[at], far_cd[at])[part // 2])
            lo, hi = sides(held[0], held[1], even_y)
            low.append(lo)
            high.append(hi)
        for p in range(PLANES):
            right = take(high, p, 0)
            left = take(low, p, LANES - WIDTH)
            l0[p, 2, to, :] = jnp.where(
                lane < WIDTH, right, jnp.where(lane >= LANES - WIDTH, left, 0.0)
            )

    for ref in (l0, l1, l2):
        zero_pads(ref, (KX, KX + 1, U, U + 1))
    for ref in (ua,):
        zero_pads(ref, (0, 1))

    levels = (l0, l1, l2)
    for depth, level in enumerate(levels):
        step = 1 << depth
        count = level.shape[2] - 2 * PAD
        starts = range(PAD, PAD + count, 8)
        if depth:
            for r0 in starts:
                f, kx, ky, surf_kz = coarse_block(
                    levels[depth - 1], rr, step // 2, PAD + 2 * (r0 - PAD), 8
                )
                put(level, F, r0, f)
                put(level, KX, r0, kx)
                put(level, KY, r0, ky)
                put(level, S, r0, surf_kz)
            if count * 2 + 2 * PAD > 0:
                put(ua, 0, PAD + count, jnp.zeros((2, 3, PAD, LANES), jnp.float32))
        for r0 in starts:
            w = weight(
                rows_of(level, KX, 2, r0),
                rows_of(level, KX, 2, r0 - 1),
                rows_of(level, KY, 2, r0),
                rows_of(level, KZ, 1, r0),
                rows_of(level, S, 2, r0),
                step,
            )
            put(level, W, r0, w)
            put(ua, 0, r0, w * rows_of(level, F, 2, r0))
        for r0 in starts:
            u, r = block_residual(level, ua, 0, step, r0)
            put(level, U, r0, u + rows_of(level, W, 2, r0) * r)
        for r0 in starts:
            put(rr, 0, r0, block_residual(level, level, U, step, r0)[1])

    own = l2.shape[2] // 2 - 4
    f, kx, ky, surf_kz = coarse_block(l2, rr, 4, own, 8)
    nine = jnp.concatenate([f, kx, ky, surf_kz], axis=0)
    place = lax.broadcasted_iota(jnp.int32, (8, LANES), 0)
    cell = lane % 32
    index = cell * 8 % LANES
    mine = place == (lane // 32 + lax.axis_index("gy")) % 4
    total = jnp.zeros((PLANES, LANES), jnp.float32)
    for r in range(4):
        for c in range(2):
            src = lax.broadcasted_iota(jnp.int32, (LANES, LANES), 0) + c * LANES
            dst = lax.broadcasted_iota(jnp.int32, (LANES, LANES), 1)
            group = (dst // 32 + lax.axis_index("gy")) % 4
            pick = jnp.where((src == dst % 32 * 8) & (group == r), 1.0, 0.0)
            total = total + jnp.dot(
                nine[:, c, r, :],
                pick,
                precision=lax.Precision.HIGHEST,
                preferred_element_type=jnp.float32,
            )
    for p in range(PLANES):
        at = slice(p * LANES, (p + 1) * LANES)
        pack_ref[:, :, at] = jnp.broadcast_to(
            total[p : p + 1][None], (pack_ref.shape[0], 1, LANES)
        )


def scaled(level, weights, step):
    f, kx, kx_lo, ky, kz, surf = level
    faces = (f, kx, kx_lo, ky, from_left(ky, step), kz)
    return tuple(weights * x for x in faces)


def whole_sweep(faces, u, step):
    f, up, down, right, left, across = faces
    rows = u.shape[2]
    other = jnp.concatenate([u[1:2], u[0:1]], axis=0)
    near = ((1.0 - damping) * u + f) + across * other
    along = up * pltpu.roll(u, rows - 1, 2) + down * pltpu.roll(u, 1, 2)
    return near + along + (right * from_right(u, step) + left * from_left(u, step))


def whole_residual(level, u, step):
    f, kx, kx_lo, ky, kz, surf = level
    rows = u.shape[2]
    return residual_of(
        f, u, pltpu.roll(u, rows - 1, 2), pltpu.roll(u, 1, 2), kx, kx_lo, ky, kz, surf, step
    )


def up_kernel(nx, ny, x_ref, l0, l1, l2, p_ref, r_ref, g3, g4, g5, ub, uc):
    me_x = lax.axis_index("gx")
    me_y = lax.axis_index("gy")
    tiles = ny // 4
    rows3 = nx * 4

    lane = lane_iota((rows3, LANES))
    row = lax.broadcasted_iota(jnp.int32, (rows3, LANES), 0)
    to_row = row % 8 // 4 * 4 + (row - lane // 32 + 4) % 4
    to_lane = (row - lane // 32 + 4) % 4 * 32 + lane % 32
    for p in range(PLANES):
        for q in range(tiles):
            if tiles == 1:
                x = x_ref[pl.ds(p, rows3, stride=PLANES), :]
            else:
                x = jnp.concatenate(
                    [
                        x_ref[pl.ds((i * ny + 4 * q) * PLANES + p, 4, stride=PLANES), :]
                        for i in range(nx)
                    ],
                    axis=0,
                )
            out = lane_take(row_take(x, to_row), to_lane)
            g3[p, q, :, :] = out

    def gathered(ref):
        kx = ref[KX : KX + 2]
        return (
            ref[F : F + 2],
            kx,
            pltpu.roll(kx, 1, 2),
            ref[KY : KY + 2],
            ref[KZ : KZ + 1],
            ref[S : S + 2],
        )

    level3 = gathered(g3)
    w3 = weight(*level3[1:], 1)
    faces3 = scaled(level3, w3, 1)
    u3 = whole_sweep(faces3, faces3[0], 1)
    g4[0:2] = whole_residual(level3, u3, 1)
    f, kx, ky, surf_kz = coarse_block(g3, g4, 1, 0, rows3 // 2)
    level4 = (f, kx, pltpu.roll(kx, 1, 2), ky, surf_kz[2:3], surf_kz[0:2])
    w4 = weight(*level4[1:], 2)
    faces4 = scaled(level4, w4, 2)
    u4 = faces4[0]
    for sweep in range(CSWEEPS - 1):
        u4 = whole_sweep(faces4, u4, 2)
    rc = whole_residual(level4, u4, 2)
    even = lane_iota(u4.shape) % 2 == 0

    def total(x):
        x = jnp.sum(jnp.where(even, x, 0.0), axis=(0, 1))
        return jnp.sum(jnp.sum(x, axis=0, keepdims=True), axis=1, keepdims=True)

    e4 = u4 + (total(rc) / total(level4[5]))[None, None]
    e4 = jnp.where(even, e4, from_left(e4, 1))
    put_strided(g4, 0, 0, e4)
    put_strided(g4, 0, 1, e4)
    u3 = u3 + g4[0:2]
    for sweep in range(POST):
        u3 = whole_sweep(faces3, u3, 1)

    rows2 = l2.shape[2] - 2 * PAD
    margin = jnp.zeros((2, tiles, PAD, LANES), jnp.float32)
    g5[:, :, 0:PAD] = margin
    g5[:, :, PAD : PAD + rows3] = u3
    g5[:, :, PAD + rows3 : 2 * PAD + rows3] = margin
    lane = lane_iota((8, LANES))
    first = me_x * 4 + PAD - 2
    skip = rows2 // 2 - 8
    for k in range(2):
        near = [g5[k, q, pl.ds(first, 8), :] for q in range(tiles)]
        for c in range(3):
            column = lane + c * LANES
            column = jnp.where(column >= 320, column - 384, column)
            coarse = (column + 64) // 8 - 8 + me_y * 32 + LANES
            index = coarse % LANES
            spread = lane_take(near[0], index)
            for q in range(1, tiles):
                spread = jnp.where(coarse // LANES == q + 1, lane_take(near[q], index), spread)
            zero = jnp.zeros((skip, LANES), jnp.float32)
            uc[k, c, PAD : PAD + skip, :] = zero
            uc[k, c, PAD + rows2 - skip : PAD + rows2, :] = zero
            for at in (PAD + skip, PAD + skip + 1):
                uc[k, c, pl.ds(at, 8, stride=2), :] = spread

    levels = (l0, l1, l2)
    zeros = jnp.zeros((2, 3, PAD, LANES), jnp.float32)
    for depth in (2, 1, 0):
        level = levels[depth]
        step = 1 << depth
        count = level.shape[2] - 2 * PAD
        margin = (24, 8, 0)[depth]
        starts = range(PAD + margin, PAD + count - margin, 8)
        for r0 in starts:
            put(uc, 0, r0, rows_of(uc, 0, 2, r0) + rows_of(level, U, 2, r0))
        for buf in (uc, ub):
            put(buf, 0, PAD + margin - 8, zeros)
            put(buf, 0, PAD + count - margin, zeros)
        for source, target in ((uc, ub), (ub, uc)):
            for r0 in starts:
                u, r = block_residual(level, source, 0, step, r0)
                put(target, 0, r0, u + rows_of(level, W, 2, r0) * r)
        if depth:
            finer = levels[depth - 1]
            need = (24, 8, 0)[depth - 1]
            half = step // 2
            first, last = need // 2, (finer.shape[2] - 2 * PAD - need) // 2
            blocks = []
            for r0 in range(first, last, 4):
                e = rows_of(uc, 0, 2, PAD + r0, 4)
                blocks.append(
                    jnp.where(lane_iota(e.shape) % step < half, e, from_left(e, half))
                )
            for r0, e in zip(range(first, last, 4), blocks):
                put_strided(ub, 0, PAD + 2 * r0, e)
                put_strided(ub, 0, PAD + 2 * r0 + 1, e)
            for r0 in range(PAD + need, PAD + 2 * last, 8):
                put(uc, 0, r0, rows_of(ub, 0, 2, r0))
        else:
            own = p_ref.shape[1]
            for r0 in range(0, own, 8):
                at = PAD + count // 2 - own // 2 + r0
                u, r = block_residual(level, uc, 0, step, at)
                for c in range(2):
                    p_ref[:, r0 : r0 + 8, c * LANES : (c + 1) * LANES] = u[:, c]
                    r_ref[:, r0 : r0 + 8, c * LANES : (c + 1) * LANES] = r[:, c]


def shape_of(*shape):
    return jax.ShapeDtypeStruct(shape, jnp.float32)


def vmem(*shape):
    return pltpu.VMEM(shape, jnp.float32)


def on_device(source, coef_x, coef_y, coef_z, surface):
    rows, cols = source.shape[1], source.shape[2]
    nx, ny = lax.axis_size("gx"), lax.axis_size("gy")
    params = pltpu.CompilerParams(vmem_limit_bytes=24 * 1024 * 1024)
    packed, strip_c, strip_d = pl.pallas_call(
        pack_kernel,
        out_shape=(shape_of(PLANES, rows, cols),) + (shape_of(rows, 2 * LANES),) * 2,
        in_specs=[pl.BlockSpec(memory_space=pltpu.HBM)] * 5,
        scratch_shapes=[pltpu.SemaphoreType.DMA((5,))],
        compiler_params=params,
        name="pack",
    )(
        *(
            pltpu.with_memory_space_constraint(x, pltpu.HBM)
            for x in (source, coef_x, coef_y, surface, coef_z)
        )
    )

    strip_c = pair_permute(strip_c, "gy", 0)
    strip_d = pair_permute(strip_d, "gy", 1, wrap=True)
    far = far_permute(packed)
    near = pair_permute(packed, "gx", 0)
    strips = jnp.concatenate([strip_d, strip_c], axis=0)
    far_strips = far_permute(strips)
    near_strips = pair_permute(strips, "gx", 0)

    heights = [3 * rows // (1 << depth) + 2 * PAD for depth in range(3)]
    planes = U + 2
    l0, l1, l2, pack = pl.pallas_call(
        down_kernel,
        out_shape=tuple(shape_of(planes, 3, h, LANES) for h in heights)
        + (shape_of(nx * ny, 1, PACK),),
        scratch_shapes=[vmem(2, 3, heights[0], LANES)] * 2,
        compiler_params=params,
        name="down",
    )(packed, near, far, strips, near_strips, far_strips)

    everyone = lax.all_to_all(pack, ("gx", "gy"), 0, 0, tiled=True)
    everyone = everyone.reshape(nx * ny * PLANES, LANES)

    tiles = ny // 4
    pressure, residual = pl.pallas_call(
        functools.partial(up_kernel, nx, ny),
        out_shape=(shape_of(*source.shape),) * 2,
        scratch_shapes=[
            vmem(PLANES, tiles, nx * 4, LANES),
            vmem(2, tiles, nx * 4, LANES),
            vmem(2, tiles, nx * 4 + 2 * PAD, LANES),
            vmem(2, 3, heights[0], LANES),
            vmem(2, 3, heights[0], LANES),
        ],
        compiler_params=params,
        name="up",
    )(everyone, l0, l1, l2)
    return pressure, residual


def solution(mesh):
    layered, plane = P(None, "gx", "gy"), P("gx", "gy")
    return jax.shard_map(
        on_device,
        mesh=mesh,
        in_specs=(layered, layered, layered, plane, layered),
        out_specs=(layered, layered),
        check_vma=False,
    )
```

```python
import functools

import jax
import jax.numpy as jnp
from jax import lax
from jax.experimental import pallas as pl
from jax.experimental.pallas import tpu as pltpu
from jax.sharding import PartitionSpec as P

LEVELS = 4
PRE = 2
POST = 2
CSWEEPS = 8
damping = 0.8

LANES = 128
WIDTH = 28
PAD = 8
PLANES = 9
PACK = PLANES * LANES
F, KX, KY, S, KZ = 0, 2, 4, 6, 8
W, U = 9, 11


def pair_permute(x, axis, first, wrap=False):
    count = lax.axis_size(axis)
    pairs = []
    for i in range(first, count if wrap else count - 1, 2):
        pairs += [(i, (i + 1) % count), ((i + 1) % count, i)]
    return lax.ppermute(x, axis, pairs)


def far_permute(x):
    nx, ny = lax.axis_size("gx"), lax.axis_size("gy")
    pairs = []
    for i in range(nx):
        for j in range(ny):
            to = (i, j ^ 2) if i in (0, nx - 1) else (((i - 1) ^ 1) + 1, j)
            pairs.append((i * ny + j, to[0] * ny + to[1]))
    return lax.ppermute(x, ("gx", "gy"), pairs)


def lane_iota(shape):
    return lax.broadcasted_iota(jnp.int32, shape, len(shape) - 1)


def from_right(x, step):
    rolled = pltpu.roll(x, LANES - step, x.ndim - 1)
    if x.shape[1] == 1:
        return rolled
    after = jnp.concatenate([rolled[:, 1:], rolled[:, :1]], axis=1)
    return jnp.where(lane_iota(x.shape) >= LANES - step, after, rolled)


def from_left(x, step):
    rolled = pltpu.roll(x, step, x.ndim - 1)
    if x.shape[1] == 1:
        return rolled
    before = jnp.concatenate([rolled[:, -1:], rolled[:, :-1]], axis=1)
    return jnp.where(lane_iota(x.shape) < step, before, rolled)


def weight(kx, kx_lo, ky, kz, surf, step):
    diag = surf + kx + kx_lo + ky + from_left(ky, step) + kz
    return jnp.where(diag > 0.0, damping / jnp.where(diag > 0.0, diag, 1.0), 0.0)


def residual_of(f, u, u_up, u_dn, kx, kx_lo, ky, kz, surf, step):
    flux = ky * (u - from_right(u, step))
    vert = kz * (u[0:1] - u[1:2])
    out = surf * u + kx * (u - u_up) + kx_lo * (u - u_dn)
    out = out + flux - from_left(flux, step)
    return f - (out + jnp.concatenate([vert, -vert], axis=0))


def lane_take(x, index):
    parts = [
        jnp.take_along_axis(x[r : r + 8], index[r : r + 8], axis=1, mode="promise_in_bounds")
        for r in range(0, x.shape[0], 8)
    ]
    return parts[0] if len(parts) == 1 else jnp.concatenate(parts, axis=0)


def row_take(x, index):
    parts = [
        jnp.take_along_axis(x[r : r + 8], index[r : r + 8], axis=0, mode="promise_in_bounds")
        for r in range(0, x.shape[0], 8)
    ]
    return parts[0] if len(parts) == 1 else jnp.concatenate(parts, axis=0)


def rows_of(ref, plane, count, start, size=8):
    return ref[plane : plane + count, :, start : start + size, :]


def block_residual(level, u_ref, u_at, step, r0):
    u = rows_of(u_ref, u_at, 2, r0)
    return u, residual_of(
        rows_of(level, F, 2, r0),
        u,
        rows_of(u_ref, u_at, 2, r0 + 1),
        rows_of(u_ref, u_at, 2, r0 - 1),
        rows_of(level, KX, 2, r0),
        rows_of(level, KX, 2, r0 - 1),
        rows_of(level, KY, 2, r0),
        rows_of(level, KZ, 1, r0),
        rows_of(level, S, 2, r0),
        step,
    )


def put(ref, plane, r0, value):
    ref[plane : plane + value.shape[0], :, r0 : r0 + value.shape[2], :] = value


def strided(ref, plane, count, start, size):
    tiles = ref.shape[1]
    return jnp.stack(
        [
            jnp.stack([ref[plane + p, c, pl.ds(start, size, stride=2), :] for c in range(tiles)])
            for p in range(count)
        ]
    )


def put_strided(ref, plane, start, value):
    for p in range(value.shape[0]):
        for c in range(value.shape[1]):
            ref[plane + p, c, pl.ds(start, value.shape[2], stride=2), :] = value[p, c]


def coarse_block(fine, resid, step, fine_row, size):
    def both(ref, plane, count):
        return strided(ref, plane, count, fine_row, size) + strided(
            ref, plane, count, fine_row + 1, size
        )

    f = both(resid, 0, 2)
    kx = strided(fine, KX, 2, fine_row + 1, size)
    ky = both(fine, KY, 2)
    surf_kz = both(fine, S, 3)
    summed = jnp.concatenate([f, kx, surf_kz], axis=0)
    summed = summed + from_right(summed, step)
    return summed[0:2], summed[2:4], from_right(ky, step), summed[4:7]


def blocks(own, count, halo):
    more = -(-halo // 8) * 8
    return range(own - more, own + count + more, 8)


def sides(mine, other, is_even):
    low = jnp.where(is_even, other, mine)
    high = jnp.where(is_even, mine, other)
    return low, high


def sides_x(near, far):
    me = lax.axis_index("gx")
    low, high = sides(near, far, lax.rem(me, 2) == 0)
    return jnp.where(me == 0, 0.0, low), high


def pack_kernel(source, coef_x, coef_y, surface, coef_z, out, c_ref, d_ref, sems):
    inputs = ((source, F, 2), (coef_x, KX, 2), (coef_y, KY, 2), (surface, S, 2), (coef_z, KZ, 0))
    copies = []
    for k, (ref, plane, count) in enumerate(inputs):
        to = out.at[plane : plane + count] if count else out.at[plane]
        copies.append(pltpu.make_async_copy(ref, to, sems.at[k]))
    for copy in copies:
        copy.start()
    for copy in copies:
        copy.wait()
    rows, cols = out.shape[1], out.shape[2]
    wall_x = lax.axis_index("gx") == lax.axis_size("gx") - 1
    wall_y = lax.axis_index("gy") == lax.axis_size("gy") - 1
    edge = out[KX : KX + 2, rows - 8 :, :]
    row = lax.broadcasted_iota(jnp.int32, edge.shape, 1)
    out[KX : KX + 2, rows - 8 :, :] = jnp.where(wall_x & (row == 7), 0.0, edge)
    edge = out[KY : KY + 2, :, cols - LANES :]
    out[KY : KY + 2, :, cols - LANES :] = jnp.where(
        wall_y & (lane_iota(edge.shape) == LANES - 1), 0.0, edge
    )

    even_y = lax.rem(lax.axis_index("gy"), 2) == 0
    lane = lane_iota((8, LANES))
    for r0 in range(0, rows, 8):
        left = [jnp.zeros((8, LANES), jnp.float32)] * 2
        right = list(left)
        for p in range(PLANES):
            begin = p * WIDTH
            for tiles, column, offset in ((left, 0, 0), (right, cols - LANES, LANES - WIDTH)):
                piece = out[p, r0 : r0 + 8, column : column + LANES]
                rolled = pltpu.roll(piece, (begin - offset) % LANES, 1)
                for a in range(2):
                    lo, hi = begin - a * LANES, begin + WIDTH - a * LANES
                    if hi > 0 and lo < LANES:
                        tiles[a] = jnp.where((lane >= lo) & (lane < hi), rolled, tiles[a])
        for a in range(2):
            at = (slice(r0, r0 + 8), slice(a * LANES, (a + 1) * LANES))
            c_ref[at] = jnp.where(even_y, right[a], left[a])
            d_ref[at] = jnp.where(even_y, left[a], right[a])


def down_kernel(
    own_ref, near_ref, far_ref, own_cd, near_cd, far_cd, l0, l1, l2, pack_ref, ua, rr, row9
):
    even_y = lax.rem(lax.axis_index("gy"), 2) == 0
    rows = own_ref.shape[1]
    lane = lane_iota((8, LANES))

    def take(tiles, p, offset):
        begin = p * WIDTH
        a, b = begin // LANES, (begin + WIDTH - 1) // LANES
        piece = tiles[a]
        if a != b:
            piece = jnp.where(lane < begin + WIDTH - b * LANES, tiles[b], tiles[a])
        return pltpu.roll(piece, (offset - begin) % LANES, 1)

    for block in range(3 * rows // 8):
        part, r0 = divmod(block * 8, rows)
        to = slice(PAD + block * 8, PAD + block * 8 + 8)
        for p in range(PLANES):
            for c in range(2):
                at = (p, slice(r0, r0 + 8), slice(c * LANES, (c + 1) * LANES))
                if part == 1:
                    l0[p, c, to, :] = own_ref[at]
                else:
                    l0[p, c, to, :] = sides_x(near_ref[at], far_ref[at])[part // 2]
        low, high = [], []
        for a in range(2):
            held = []
            for base in (rows, 0):
                at = (slice(base + r0, base + r0 + 8), slice(a * LANES, (a + 1) * LANES))
                if part == 1:
                    held.append(own_cd[at])
                else:
                    held.append(sides_x(near_cd[at], far_cd[at])[part // 2])
            lo, hi = sides(held[0], held[1], even_y)
            low.append(lo)
            high.append(hi)
        for p in range(PLANES):
            right = take(high, p, 0)
            left = take(low, p, LANES - WIDTH)
            l0[p, 2, to, :] = jnp.where(
                lane < WIDTH, right, jnp.where(lane >= LANES - WIDTH, left, 0.0)
            )

    halos = ((26, 25, 24), (12, 11, 10), (5, 4, 0))
    levels = (l0, l1, l2)
    for depth, level in enumerate(levels):
        step = 1 << depth
        count = (level.shape[2] - 2 * PAD) // 3
        first, second, last = (blocks(PAD + count, count, halo) for halo in halos[depth])
        if depth:
            for r0 in range(PAD, PAD + 3 * count, 8):
                f, kx, ky, surf_kz = coarse_block(
                    levels[depth - 1], rr, step // 2, PAD + 2 * (r0 - PAD), 8
                )
                put(level, F, r0, f)
                put(level, KX, r0, kx)
                put(level, KY, r0, ky)
                put(level, S, r0, surf_kz)
        for r0 in first:
            w = weight(
                rows_of(level, KX, 2, r0),
                rows_of(level, KX, 2, r0 - 1),
                rows_of(level, KY, 2, r0),
                rows_of(level, KZ, 1, r0),
                rows_of(level, S, 2, r0),
                step,
            )
            put(level, W, r0, w)
            put(ua, 0, r0, w * rows_of(level, F, 2, r0))
        for r0 in second:
            u, r = block_residual(level, ua, 0, step, r0)
            put(level, U, r0, u + rows_of(level, W, 2, r0) * r)
        for r0 in last:
            put(rr, 0, r0, block_residual(level, level, U, step, r0)[1])

    own = l2.shape[2] // 2 - 4
    f, kx, ky, surf_kz = coarse_block(l2, rr, 4, own, 8)
    nine = jnp.concatenate([f, kx, ky, surf_kz], axis=0)
    place = lax.broadcasted_iota(jnp.int32, (8, LANES), 0)
    cell = lane % 32
    index = cell * 8 % LANES
    mine = place == (lane // 32 + lax.axis_index("gy")) % 4
    total = jnp.zeros((PLANES, LANES), jnp.float32)
    for r in range(4):
        for c in range(2):
            src = lax.broadcasted_iota(jnp.int32, (LANES, LANES), 0) + c * LANES
            dst = lax.broadcasted_iota(jnp.int32, (LANES, LANES), 1)
            group = (dst // 32 + lax.axis_index("gy")) % 4
            pick = jnp.where((src == dst % 32 * 8) & (group == r), 1.0, 0.0)
            total = total + jnp.dot(
                nine[:, c, r, :],
                pick,
                precision=lax.Precision.HIGHEST,
                preferred_element_type=jnp.float32,
            )
    row9[0:PLANES] = total
    row9[PLANES : 2 * PLANES] = total
    for r0 in range(0, pack_ref.shape[0], 8):
        pack_ref[r0 : r0 + 8] = row9[r0 % PLANES : r0 % PLANES + 8]


def scaled(level, weights, step):
    f, kx, kx_lo, ky, kz, surf = level
    faces = (f, kx, kx_lo, ky, from_left(ky, step), kz)
    return tuple(weights * x for x in faces)


def whole_sweep(faces, u, step):
    f, up, down, right, left, across = faces
    rows = u.shape[2]
    other = jnp.concatenate([u[1:2], u[0:1]], axis=0)
    near = ((1.0 - damping) * u + f) + across * other
    along = up * pltpu.roll(u, rows - 1, 2) + down * pltpu.roll(u, 1, 2)
    return near + along + (right * from_right(u, step) + left * from_left(u, step))


def whole_residual(level, u, step):
    f, kx, kx_lo, ky, kz, surf = level
    rows = u.shape[2]
    return residual_of(
        f, u, pltpu.roll(u, rows - 1, 2), pltpu.roll(u, 1, 2), kx, kx_lo, ky, kz, surf, step
    )


def up_kernel(nx, ny, x_ref, l0, l1, l2, p_ref, r_ref, g3, g4, g5, ub, uc, p_own, r_own, sems):
    me_x = lax.axis_index("gx")
    me_y = lax.axis_index("gy")
    tiles = ny // 4
    rows3 = nx * 4

    lane = lane_iota((rows3, LANES))
    row = lax.broadcasted_iota(jnp.int32, (rows3, LANES), 0)
    to_row = row % 8 // 4 * 4 + (row - lane // 32 + 4) % 4
    to_lane = (row - lane // 32 + 4) % 4 * 32 + lane % 32
    for p in range(PLANES):
        for q in range(tiles):
            if tiles == 1:
                x = x_ref[pl.ds(p, rows3, stride=PLANES), :]
            else:
                x = jnp.concatenate(
                    [
                        x_ref[pl.ds((i * ny + 4 * q) * PLANES + p, 4, stride=PLANES), :]
                        for i in range(nx)
                    ],
                    axis=0,
                )
            out = lane_take(row_take(x, to_row), to_lane)
            g3[p, q, :, :] = out

    def gathered(ref):
        kx = ref[KX : KX + 2]
        return (
            ref[F : F + 2],
            kx,
            pltpu.roll(kx, 1, 2),
            ref[KY : KY + 2],
            ref[KZ : KZ + 1],
            ref[S : S + 2],
        )

    level3 = gathered(g3)
    w3 = weight(*level3[1:], 1)
    faces3 = scaled(level3, w3, 1)
    u3 = whole_sweep(faces3, faces3[0], 1)
    g4[0:2] = whole_residual(level3, u3, 1)
    f, kx, ky, surf_kz = coarse_block(g3, g4, 1, 0, rows3 // 2)
    level4 = (f, kx, pltpu.roll(kx, 1, 2), ky, surf_kz[2:3], surf_kz[0:2])
    w4 = weight(*level4[1:], 2)
    faces4 = scaled(level4, w4, 2)
    u4 = faces4[0]
    for sweep in range(CSWEEPS - 1):
        u4 = whole_sweep(faces4, u4, 2)
    rc = whole_residual(level4, u4, 2)
    even = lane_iota(u4.shape) % 2 == 0

    def total(x):
        x = jnp.sum(jnp.where(even, x, 0.0), axis=(0, 1))
        return jnp.sum(jnp.sum(x, axis=0, keepdims=True), axis=1, keepdims=True)

    shift = (total(rc) / total(level4[5]))[None, None]
    spread4 = jnp.where(even, u4, from_left(u4, 1))
    put_strided(g4, 0, 0, spread4)
    put_strided(g4, 0, 1, spread4)
    u3 = (u3 + g4[0:2]) + shift
    for sweep in range(POST):
        u3 = whole_sweep(faces3, u3, 1)

    rows2 = l2.shape[2] - 2 * PAD
    margin = jnp.zeros((2, tiles, PAD, LANES), jnp.float32)
    g5[:, :, 0:PAD] = margin
    g5[:, :, PAD : PAD + rows3] = u3
    g5[:, :, PAD + rows3 : 2 * PAD + rows3] = margin
    lane = lane_iota((8, LANES))
    first = me_x * 4 + PAD - 2
    skip = rows2 // 2 - 8
    for k in range(2):
        near = [g5[k, q, pl.ds(first, 8), :] for q in range(tiles)]
        for c in range(3):
            column = lane + c * LANES
            column = jnp.where(column >= 320, column - 384, column)
            coarse = (column + 64) // 8 - 8 + me_y * 32 + LANES
            index = coarse % LANES
            spread = lane_take(near[0], index)
            for q in range(1, tiles):
                spread = jnp.where(coarse // LANES == q + 1, lane_take(near[q], index), spread)
            for at in (PAD + skip, PAD + skip + 1):
                uc[k, c, pl.ds(at, 8, stride=2), :] = spread

    levels = (l0, l1, l2)
    for depth in (2, 1, 0):
        level = levels[depth]
        step = 1 << depth
        count = (level.shape[2] - 2 * PAD) // 3
        own = PAD + count
        starts = blocks(own, count, 4)
        for r0 in starts:
            put(uc, 0, r0, rows_of(uc, 0, 2, r0) + rows_of(level, U, 2, r0))
        for source, target in ((uc, ub), (ub, uc)):
            for r0 in starts:
                u, r = block_residual(level, source, 0, step, r0)
                put(target, 0, r0, u + rows_of(level, W, 2, r0) * r)
        if depth:
            half = step // 2
            finer = PAD + 2 * count - 4
            spread = []
            for r0 in range(own - 2, own + count + 2, 4):
                e = rows_of(uc, 0, 2, r0, 4)
                spread.append(
                    jnp.where(lane_iota(e.shape) % step < half, e, from_left(e, half))
                )
            for k, e in enumerate(spread):
                put_strided(ub, 0, finer + 8 * k, e)
                put_strided(ub, 0, finer + 8 * k + 1, e)
            for k in range(len(spread)):
                put(uc, 0, finer + 8 * k, rows_of(ub, 0, 2, finer + 8 * k))
        else:
            for r0 in range(0, count, 8):
                u = rows_of(uc, 0, 2, own + r0)
                for c in range(2):
                    p_own[:, r0 : r0 + 8, c * LANES : (c + 1) * LANES] = u[:, c]
            copy_p = pltpu.make_async_copy(p_own, p_ref, sems.at[0])
            copy_p.start()
            for r0 in range(0, count, 8):
                r = block_residual(level, uc, 0, step, own + r0)[1]
                for c in range(2):
                    r_own[:, r0 : r0 + 8, c * LANES : (c + 1) * LANES] = r[:, c]
            copy_r = pltpu.make_async_copy(r_own, r_ref, sems.at[1])
            copy_r.start()
            copy_p.wait()
            copy_r.wait()


def shape_of(*shape):
    return jax.ShapeDtypeStruct(shape, jnp.float32)


def vmem(*shape):
    return pltpu.VMEM(shape, jnp.float32)


def on_device(source, coef_x, coef_y, coef_z, surface):
    rows, cols = source.shape[1], source.shape[2]
    nx, ny = lax.axis_size("gx"), lax.axis_size("gy")
    params = pltpu.CompilerParams(vmem_limit_bytes=24 * 1024 * 1024)
    packed, strip_c, strip_d = pl.pallas_call(
        pack_kernel,
        out_shape=(shape_of(PLANES, rows, cols),) + (shape_of(rows, 2 * LANES),) * 2,
        in_specs=[pl.BlockSpec(memory_space=pltpu.HBM)] * 5,
        scratch_shapes=[pltpu.SemaphoreType.DMA((5,))],
        compiler_params=params,
        name="pack",
    )(
        *(
            pltpu.with_memory_space_constraint(x, pltpu.HBM)
            for x in (source, coef_x, coef_y, surface, coef_z)
        )
    )

    strip_c = pair_permute(strip_c, "gy", 0)
    strip_d = pair_permute(strip_d, "gy", 1, wrap=True)
    far = far_permute(packed)
    near = pair_permute(packed, "gx", 0)
    strips = jnp.concatenate([strip_d, strip_c], axis=0)
    far_strips = far_permute(strips)
    near_strips = pair_permute(strips, "gx", 0)

    heights = [3 * rows // (1 << depth) + 2 * PAD for depth in range(3)]
    planes = U + 2
    l0, l1, l2, pack = pl.pallas_call(
        down_kernel,
        out_shape=tuple(shape_of(planes, 3, h, LANES) for h in heights)
        + (shape_of(nx * ny * PLANES, LANES),),
        scratch_shapes=[vmem(2, 3, heights[0], LANES)] * 2 + [vmem(24, LANES)],
        compiler_params=params,
        name="down",
    )(packed, near, far, strips, near_strips, far_strips)

    everyone = lax.all_to_all(
        pack.reshape(nx * ny, 1, PACK), ("gx", "gy"), 0, 0, tiled=True
    )
    everyone = everyone.reshape(nx * ny * PLANES, LANES)

    tiles = ny // 4
    pressure, residual = pl.pallas_call(
        functools.partial(up_kernel, nx, ny),
        out_shape=(shape_of(*source.shape),) * 2,
        scratch_shapes=[
            vmem(PLANES, tiles, nx * 4, LANES),
            vmem(2, tiles, nx * 4, LANES),
            vmem(2, tiles, nx * 4 + 2 * PAD, LANES),
            vmem(2, 3, heights[0], LANES),
            vmem(2, 3, heights[0], LANES),
            vmem(*source.shape),
            vmem(*source.shape),
            pltpu.SemaphoreType.DMA((2,)),
        ],
        out_specs=[pl.BlockSpec(memory_space=pltpu.HBM)] * 2,
        compiler_params=params,
        name="up",
    )(everyone, l0, l1, l2)
    return pressure, residual


def solution(mesh):
    layered, plane = P(None, "gx", "gy"), P("gx", "gy")
    return jax.shard_map(
        on_device,
        mesh=mesh,
        in_specs=(layered, layered, layered, plane, layered),
        out_specs=(layered, layered),
        check_vma=False,
    )
```

```python
import functools

import jax
import jax.numpy as jnp
from jax import lax
from jax.experimental import pallas as pl
from jax.experimental.pallas import tpu as pltpu
from jax.sharding import PartitionSpec as P

LEVELS = 4
PRE = 2
POST = 2
CSWEEPS = 8
damping = 0.8

LANES = 128
WIDTH = 28
PAD = 8
PLANES = 9
PACK = PLANES * LANES
F, KX, KY, S, KZ = 0, 2, 4, 6, 8
W, U = 9, 11


def pair_permute(x, axis, first, wrap=False):
    count = lax.axis_size(axis)
    pairs = []
    for i in range(first, count if wrap else count - 1, 2):
        pairs += [(i, (i + 1) % count), ((i + 1) % count, i)]
    return lax.ppermute(x, axis, pairs)


def far_permute(x):
    nx, ny = lax.axis_size("gx"), lax.axis_size("gy")
    pairs = []
    for i in range(nx):
        for j in range(ny):
            to = (i, j ^ 2) if i in (0, nx - 1) else (((i - 1) ^ 1) + 1, j)
            pairs.append((i * ny + j, to[0] * ny + to[1]))
    return lax.ppermute(x, ("gx", "gy"), pairs)


def lane_iota(shape):
    return lax.broadcasted_iota(jnp.int32, shape, len(shape) - 1)


def from_right(x, step):
    rolled = pltpu.roll(x, LANES - step, x.ndim - 1)
    if x.shape[1] == 1:
        return rolled
    after = jnp.concatenate([rolled[:, 1:], rolled[:, :1]], axis=1)
    return jnp.where(lane_iota(x.shape) >= LANES - step, after, rolled)


def from_left(x, step):
    rolled = pltpu.roll(x, step, x.ndim - 1)
    if x.shape[1] == 1:
        return rolled
    before = jnp.concatenate([rolled[:, -1:], rolled[:, :-1]], axis=1)
    return jnp.where(lane_iota(x.shape) < step, before, rolled)


def weight(kx, kx_lo, ky, kz, surf, step):
    diag = surf + kx + kx_lo + ky + from_left(ky, step) + kz
    return jnp.where(diag > 0.0, damping / jnp.where(diag > 0.0, diag, 1.0), 0.0)


def residual_of(f, u, u_up, u_dn, kx, kx_lo, ky, kz, surf, step):
    flux = ky * (u - from_right(u, step))
    vert = kz * (u[0:1] - u[1:2])
    out = surf * u + kx * (u - u_up) + kx_lo * (u - u_dn)
    out = out + flux - from_left(flux, step)
    return f - (out + jnp.concatenate([vert, -vert], axis=0))


def lane_take(x, index):
    parts = [
        jnp.take_along_axis(x[r : r + 8], index[r : r + 8], axis=1, mode="promise_in_bounds")
        for r in range(0, x.shape[0], 8)
    ]
    return parts[0] if len(parts) == 1 else jnp.concatenate(parts, axis=0)


def row_take(x, index):
    parts = [
        jnp.take_along_axis(x[r : r + 8], index[r : r + 8], axis=0, mode="promise_in_bounds")
        for r in range(0, x.shape[0], 8)
    ]
    return parts[0] if len(parts) == 1 else jnp.concatenate(parts, axis=0)


def rows_of(ref, plane, count, start, size=8):
    return ref[plane : plane + count, :, start : start + size, :]


def block_residual(level, u_ref, u_at, step, r0):
    u = rows_of(u_ref, u_at, 2, r0)
    return u, residual_of(
        rows_of(level, F, 2, r0),
        u,
        rows_of(u_ref, u_at, 2, r0 + 1),
        rows_of(u_ref, u_at, 2, r0 - 1),
        rows_of(level, KX, 2, r0),
        rows_of(level, KX, 2, r0 - 1),
        rows_of(level, KY, 2, r0),
        rows_of(level, KZ, 1, r0),
        rows_of(level, S, 2, r0),
        step,
    )


def put(ref, plane, r0, value):
    ref[plane : plane + value.shape[0], :, r0 : r0 + value.shape[2], :] = value


def strided(ref, plane, count, start, size):
    tiles = ref.shape[1]
    return jnp.stack(
        [
            jnp.stack([ref[plane + p, c, pl.ds(start, size, stride=2), :] for c in range(tiles)])
            for p in range(count)
        ]
    )


def put_strided(ref, plane, start, value):
    for p in range(value.shape[0]):
        for c in range(value.shape[1]):
            ref[plane + p, c, pl.ds(start, value.shape[2], stride=2), :] = value[p, c]


def coarse_block(fine, resid, step, fine_row, size):
    def both(ref, plane, count):
        return strided(ref, plane, count, fine_row, size) + strided(
            ref, plane, count, fine_row + 1, size
        )

    f = both(resid, 0, 2)
    kx = strided(fine, KX, 2, fine_row + 1, size)
    ky = both(fine, KY, 2)
    surf_kz = both(fine, S, 3)
    summed = jnp.concatenate([f, kx, surf_kz], axis=0)
    summed = summed + from_right(summed, step)
    return summed[0:2], summed[2:4], from_right(ky, step), summed[4:7]


def blocks(own, count, halo):
    more = -(-halo // 8) * 8
    return range(own - more, own + count + more, 8)


def sides(mine, other, is_even):
    low = jnp.where(is_even, other, mine)
    high = jnp.where(is_even, mine, other)
    return low, high


def sides_x(near, far):
    me = lax.axis_index("gx")
    low, high = sides(near, far, lax.rem(me, 2) == 0)
    return jnp.where(me == 0, 0.0, low), high


def pack_kernel(source, coef_x, coef_y, surface, coef_z, out, c_ref, d_ref, sems):
    inputs = ((source, F, 2), (coef_x, KX, 2), (coef_y, KY, 2), (surface, S, 2), (coef_z, KZ, 0))
    copies = []
    for k, (ref, plane, count) in enumerate(inputs):
        to = out.at[plane : plane + count] if count else out.at[plane]
        copies.append(pltpu.make_async_copy(ref, to, sems.at[k]))
    for copy in copies:
        copy.start()
    for copy in copies:
        copy.wait()
    rows, cols = out.shape[1], out.shape[2]
    wall_x = lax.axis_index("gx") == lax.axis_size("gx") - 1
    wall_y = lax.axis_index("gy") == lax.axis_size("gy") - 1
    edge = out[KX : KX + 2, rows - 8 :, :]
    row = lax.broadcasted_iota(jnp.int32, edge.shape, 1)
    out[KX : KX + 2, rows - 8 :, :] = jnp.where(wall_x & (row == 7), 0.0, edge)
    edge = out[KY : KY + 2, :, cols - LANES :]
    out[KY : KY + 2, :, cols - LANES :] = jnp.where(
        wall_y & (lane_iota(edge.shape) == LANES - 1), 0.0, edge
    )

    even_y = lax.rem(lax.axis_index("gy"), 2) == 0
    lane = lane_iota((8, LANES))
    for r0 in range(0, rows, 8):
        left = [jnp.zeros((8, LANES), jnp.float32)] * 2
        right = list(left)
        for p in range(PLANES):
            begin = p * WIDTH
            for tiles, column, offset in ((left, 0, 0), (right, cols - LANES, LANES - WIDTH)):
                piece = out[p, r0 : r0 + 8, column : column + LANES]
                rolled = pltpu.roll(piece, (begin - offset) % LANES, 1)
                for a in range(2):
                    lo, hi = begin - a * LANES, begin + WIDTH - a * LANES
                    if hi > 0 and lo < LANES:
                        tiles[a] = jnp.where((lane >= lo) & (lane < hi), rolled, tiles[a])
        for a in range(2):
            at = (slice(r0, r0 + 8), slice(a * LANES, (a + 1) * LANES))
            c_ref[at] = jnp.where(even_y, right[a], left[a])
            d_ref[at] = jnp.where(even_y, left[a], right[a])


def down_kernel(
    own_ref, near_ref, far_ref, own_cd, near_cd, far_cd, l0, l1, l2, pack_ref, ua, rr, row9
):
    even_y = lax.rem(lax.axis_index("gy"), 2) == 0
    rows = own_ref.shape[1]
    lane = lane_iota((8, LANES))

    def take(tiles, p, offset):
        begin = p * WIDTH
        a, b = begin // LANES, (begin + WIDTH - 1) // LANES
        piece = tiles[a]
        if a != b:
            piece = jnp.where(lane < begin + WIDTH - b * LANES, tiles[b], tiles[a])
        return pltpu.roll(piece, (offset - begin) % LANES, 1)

    for block in range(3 * rows // 8):
        part, r0 = divmod(block * 8, rows)
        to = slice(PAD + block * 8, PAD + block * 8 + 8)
        for p in range(PLANES):
            for c in range(2):
                at = (p, slice(r0, r0 + 8), slice(c * LANES, (c + 1) * LANES))
                if part == 1:
                    l0[p, c, to, :] = own_ref[at]
                else:
                    l0[p, c, to, :] = sides_x(near_ref[at], far_ref[at])[part // 2]
        low, high = [], []
        for a in range(2):
            held = []
            for base in (rows, 0):
                at = (slice(base + r0, base + r0 + 8), slice(a * LANES, (a + 1) * LANES))
                if part == 1:
                    held.append(own_cd[at])
                else:
                    held.append(sides_x(near_cd[at], far_cd[at])[part // 2])
            lo, hi = sides(held[0], held[1], even_y)
            low.append(lo)
            high.append(hi)
        for p in range(PLANES):
            right = take(high, p, 0)
            left = take(low, p, LANES - WIDTH)
            l0[p, 2, to, :] = jnp.where(
                lane < WIDTH, right, jnp.where(lane >= LANES - WIDTH, left, 0.0)
            )

    halos = ((26, 25, 24), (12, 11, 10), (5, 4, 0))
    levels = (l0, l1, l2)
    for depth, level in enumerate(levels):
        step = 1 << depth
        count = (level.shape[2] - 2 * PAD) // 3
        first, second, last = (blocks(PAD + count, count, halo) for halo in halos[depth])
        if depth:
            for r0 in range(PAD, PAD + 3 * count, 8):
                f, kx, ky, surf_kz = coarse_block(
                    levels[depth - 1], rr, step // 2, PAD + 2 * (r0 - PAD), 8
                )
                put(level, F, r0, f)
                put(level, KX, r0, kx)
                put(level, KY, r0, ky)
                put(level, S, r0, surf_kz)
        for r0 in first:
            w = weight(
                rows_of(level, KX, 2, r0),
                rows_of(level, KX, 2, r0 - 1),
                rows_of(level, KY, 2, r0),
                rows_of(level, KZ, 1, r0),
                rows_of(level, S, 2, r0),
                step,
            )
            put(level, W, r0, w)
            put(ua, 0, r0, w * rows_of(level, F, 2, r0))
        for r0 in second:
            u, r = block_residual(level, ua, 0, step, r0)
            put(level, U, r0, u + rows_of(level, W, 2, r0) * r)
        for r0 in last:
            put(rr, 0, r0, block_residual(level, level, U, step, r0)[1])

    own = l2.shape[2] // 2 - 4
    f, kx, ky, surf_kz = coarse_block(l2, rr, 4, own, 8)
    nine = jnp.concatenate([f, kx, ky, surf_kz], axis=0)
    place = lax.broadcasted_iota(jnp.int32, (8, LANES), 0)
    cell = lane % 32
    index = cell * 8 % LANES
    mine = place == (lane // 32 + lax.axis_index("gy")) % 4
    total = jnp.zeros((PLANES, LANES), jnp.float32)
    for r in range(4):
        for c in range(2):
            src = lax.broadcasted_iota(jnp.int32, (LANES, LANES), 0) + c * LANES
            dst = lax.broadcasted_iota(jnp.int32, (LANES, LANES), 1)
            group = (dst // 32 + lax.axis_index("gy")) % 4
            pick = jnp.where((src == dst % 32 * 8) & (group == r), 1.0, 0.0)
            total = total + jnp.dot(
                nine[:, c, r, :],
                pick,
                precision=lax.Precision.HIGHEST,
                preferred_element_type=jnp.float32,
            )
    row9[0:PLANES] = total
    row9[PLANES : 2 * PLANES] = total
    for r0 in range(0, pack_ref.shape[0], 8):
        pack_ref[r0 : r0 + 8] = row9[r0 % PLANES : r0 % PLANES + 8]


def scaled(level, weights, step):
    f, kx, kx_lo, ky, kz, surf = level
    faces = (f, kx, kx_lo, ky, from_left(ky, step), kz)
    return tuple(weights * x for x in faces)


def whole_sweep(faces, u, step):
    f, up, down, right, left, across = faces
    rows = u.shape[2]
    other = jnp.concatenate([u[1:2], u[0:1]], axis=0)
    near = ((1.0 - damping) * u + f) + across * other
    along = up * pltpu.roll(u, rows - 1, 2) + down * pltpu.roll(u, 1, 2)
    return near + along + (right * from_right(u, step) + left * from_left(u, step))


def whole_residual(level, u, step):
    f, kx, kx_lo, ky, kz, surf = level
    rows = u.shape[2]
    return residual_of(
        f, u, pltpu.roll(u, rows - 1, 2), pltpu.roll(u, 1, 2), kx, kx_lo, ky, kz, surf, step
    )


def up_kernel(nx, ny, x_ref, l0, l1, l2, p_ref, r_ref, g3, g4, g5, ub, uc, p_own, r_own, sems):
    me_x = lax.axis_index("gx")
    me_y = lax.axis_index("gy")
    tiles = ny // 4
    rows3 = nx * 4

    lane = lane_iota((rows3, LANES))
    row = lax.broadcasted_iota(jnp.int32, (rows3, LANES), 0)
    to_row = row % 8 // 4 * 4 + (row - lane // 32 + 4) % 4
    to_lane = (row - lane // 32 + 4) % 4 * 32 + lane % 32
    for p in range(PLANES):
        for q in range(tiles):
            if tiles == 1:
                x = x_ref[pl.ds(p, rows3, stride=PLANES), :]
            else:
                x = jnp.concatenate(
                    [
                        x_ref[pl.ds((i * ny + 4 * q) * PLANES + p, 4, stride=PLANES), :]
                        for i in range(nx)
                    ],
                    axis=0,
                )
            out = lane_take(row_take(x, to_row), to_lane)
            g3[p, q, :, :] = out

    def gathered(ref):
        kx = ref[KX : KX + 2]
        return (
            ref[F : F + 2],
            kx,
            pltpu.roll(kx, 1, 2),
            ref[KY : KY + 2],
            ref[KZ : KZ + 1],
            ref[S : S + 2],
        )

    level3 = gathered(g3)
    w3 = weight(*level3[1:], 1)
    faces3 = scaled(level3, w3, 1)
    u3 = whole_sweep(faces3, faces3[0], 1)
    g4[0:2] = whole_residual(level3, u3, 1)
    f, kx, ky, surf_kz = coarse_block(g3, g4, 1, 0, rows3 // 2)
    level4 = (f, kx, pltpu.roll(kx, 1, 2), ky, surf_kz[2:3], surf_kz[0:2])
    w4 = weight(*level4[1:], 2)
    faces4 = scaled(level4, w4, 2)
    u4 = faces4[0]
    for sweep in range(CSWEEPS - 1):
        u4 = whole_sweep(faces4, u4, 2)
    rc = whole_residual(level4, u4, 2)
    even = lane_iota(u4.shape) % 2 == 0

    def total(x):
        x = jnp.sum(jnp.where(even, x, 0.0), axis=(0, 1))
        return jnp.sum(jnp.sum(x, axis=0, keepdims=True), axis=1, keepdims=True)

    shift = (total(rc) / total(level4[5]))[None, None]
    spread4 = jnp.where(even, u4, from_left(u4, 1))
    put_strided(g4, 0, 0, spread4)
    put_strided(g4, 0, 1, spread4)
    u3 = (u3 + g4[0:2]) + shift
    for sweep in range(POST):
        u3 = whole_sweep(faces3, u3, 1)

    rows2 = l2.shape[2] - 2 * PAD
    margin = jnp.zeros((2, tiles, PAD, LANES), jnp.float32)
    g5[:, :, 0:PAD] = margin
    g5[:, :, PAD : PAD + rows3] = u3
    g5[:, :, PAD + rows3 : 2 * PAD + rows3] = margin
    lane = lane_iota((8, LANES))
    first = me_x * 4 + PAD - 2
    skip = rows2 // 2 - 8
    for k in range(2):
        near = [g5[k, q, pl.ds(first, 8), :] for q in range(tiles)]
        for c in range(3):
            column = lane + c * LANES
            column = jnp.where(column >= 320, column - 384, column)
            coarse = (column + 64) // 8 - 8 + me_y * 32 + LANES
            index = coarse % LANES
            spread = lane_take(near[0], index)
            for q in range(1, tiles):
                spread = jnp.where(coarse // LANES == q + 1, lane_take(near[q], index), spread)
            for at in (PAD + skip, PAD + skip + 1):
                uc[k, c, pl.ds(at, 8, stride=2), :] = spread

    levels = (l0, l1, l2)
    for depth in (2, 1, 0):
        level = levels[depth]
        step = 1 << depth
        count = (level.shape[2] - 2 * PAD) // 3
        own = PAD + count
        starts = blocks(own, count, 4)
        for r0 in starts:
            put(uc, 0, r0, rows_of(uc, 0, 2, r0) + rows_of(level, U, 2, r0))
        for source, target in ((uc, ub), (ub, uc)):
            for r0 in starts:
                u, r = block_residual(level, source, 0, step, r0)
                put(target, 0, r0, u + rows_of(level, W, 2, r0) * r)
        if depth:
            half = step // 2
            finer = PAD + 2 * count - 4
            spread = []
            for r0 in range(own - 2, own + count + 2, 4):
                e = rows_of(uc, 0, 2, r0, 4)
                spread.append(
                    jnp.where(lane_iota(e.shape) % step < half, e, from_left(e, half))
                )
            for k, e in enumerate(spread):
                put_strided(ub, 0, finer + 8 * k, e)
                put_strided(ub, 0, finer + 8 * k + 1, e)
            for k in range(len(spread)):
                put(uc, 0, finer + 8 * k, rows_of(ub, 0, 2, finer + 8 * k))
        else:
            for r0 in range(0, count, 8):
                u = rows_of(uc, 0, 2, own + r0)
                for c in range(2):
                    p_own[:, r0 : r0 + 8, c * LANES : (c + 1) * LANES] = u[:, c]
            copy_p = pltpu.make_async_copy(p_own, p_ref, sems.at[0])
            copy_p.start()
            for r0 in range(0, count, 8):
                r = block_residual(level, uc, 0, step, own + r0)[1]
                for c in range(2):
                    r_own[:, r0 : r0 + 8, c * LANES : (c + 1) * LANES] = r[:, c]
            copy_r = pltpu.make_async_copy(r_own, r_ref, sems.at[1])
            copy_r.start()
            copy_p.wait()
            copy_r.wait()


def shape_of(*shape):
    return jax.ShapeDtypeStruct(shape, jnp.float32)


def vmem(*shape):
    return pltpu.VMEM(shape, jnp.float32)


def on_device(source, coef_x, coef_y, coef_z, surface):
    rows, cols = source.shape[1], source.shape[2]
    nx, ny = lax.axis_size("gx"), lax.axis_size("gy")
    params = pltpu.CompilerParams(vmem_limit_bytes=24 * 1024 * 1024)
    packed, strip_c, strip_d = pl.pallas_call(
        pack_kernel,
        out_shape=(shape_of(PLANES, rows, cols),) + (shape_of(rows, 2 * LANES),) * 2,
        in_specs=[pl.BlockSpec(memory_space=pltpu.HBM)] * 5,
        scratch_shapes=[pltpu.SemaphoreType.DMA((5,))],
        compiler_params=params,
        name="pack",
    )(
        *(
            pltpu.with_memory_space_constraint(x, pltpu.HBM)
            for x in (source, coef_x, coef_y, surface, coef_z)
        )
    )

    strip_c = pair_permute(strip_c, "gy", 0)
    strip_d = pair_permute(strip_d, "gy", 1, wrap=True)
    far = far_permute(packed)
    near = pair_permute(packed, "gx", 0)
    strips = jnp.concatenate([strip_d, strip_c], axis=0)
    nil = 0.0 * lax.axis_index("gy").astype(jnp.float32)
    strips = lax.optimization_barrier(strips) + nil
    far_strips = far_permute(strips)
    near_strips = pair_permute(strips, "gx", 0)

    heights = [3 * rows // (1 << depth) + 2 * PAD for depth in range(3)]
    planes = U + 2
    l0, l1, l2, pack = pl.pallas_call(
        down_kernel,
        out_shape=tuple(shape_of(planes, 3, h, LANES) for h in heights)
        + (shape_of(nx * ny * PLANES, LANES),),
        scratch_shapes=[vmem(2, 3, heights[0], LANES)] * 2 + [vmem(24, LANES)],
        compiler_params=params,
        name="down",
    )(packed, near, far, strips, near_strips, far_strips)

    everyone = lax.all_to_all(
        pack.reshape(nx * ny, 1, PACK), ("gx", "gy"), 0, 0, tiled=True
    )
    everyone = everyone.reshape(nx * ny * PLANES, LANES)

    tiles = ny // 4
    pressure, residual = pl.pallas_call(
        functools.partial(up_kernel, nx, ny),
        out_shape=(shape_of(*source.shape),) * 2,
        scratch_shapes=[
            vmem(PLANES, tiles, nx * 4, LANES),
            vmem(2, tiles, nx * 4, LANES),
            vmem(2, tiles, nx * 4 + 2 * PAD, LANES),
            vmem(2, 3, heights[0], LANES),
            vmem(2, 3, heights[0], LANES),
            vmem(*source.shape),
            vmem(*source.shape),
            pltpu.SemaphoreType.DMA((2,)),
        ],
        out_specs=[pl.BlockSpec(memory_space=pltpu.HBM)] * 2,
        compiler_params=params,
        name="up",
    )(everyone, l0, l1, l2)
    return pressure, residual


def solution(mesh):
    layered, plane = P(None, "gx", "gy"), P("gx", "gy")
    return jax.shard_map(
        on_device,
        mesh=mesh,
        in_specs=(layered, layered, layered, plane, layered),
        out_specs=(layered, layered),
        check_vma=False,
    )
```

```python
import functools

import jax
import jax.numpy as jnp
from jax import lax
from jax.experimental import pallas as pl
from jax.experimental.pallas import tpu as pltpu
from jax.sharding import PartitionSpec as P

LEVELS = 4
PRE = 2
POST = 2
CSWEEPS = 8
damping = 0.8

LANES = 128
WIDTH = 28
PAD = 8
PLANES = 9
PACK = PLANES * LANES
F, KX, KY, S, KZ = 0, 2, 4, 6, 8
W, U = 9, 11


def pair_permute(x, axis, first, wrap=False):
    count = lax.axis_size(axis)
    pairs = []
    for i in range(first, count if wrap else count - 1, 2):
        pairs += [(i, (i + 1) % count), ((i + 1) % count, i)]
    return lax.ppermute(x, axis, pairs)


def far_permute(x):
    nx, ny = lax.axis_size("gx"), lax.axis_size("gy")
    pairs = []
    for i in range(nx):
        for j in range(ny):
            to = (i, j ^ 2) if i in (0, nx - 1) else (((i - 1) ^ 1) + 1, j)
            pairs.append((i * ny + j, to[0] * ny + to[1]))
    return lax.ppermute(x, ("gx", "gy"), pairs)


def lane_iota(shape):
    return lax.broadcasted_iota(jnp.int32, shape, len(shape) - 1)


def from_right(x, step):
    rolled = pltpu.roll(x, LANES - step, x.ndim - 1)
    if x.shape[1] == 1:
        return rolled
    after = jnp.concatenate([rolled[:, 1:], rolled[:, :1]], axis=1)
    return jnp.where(lane_iota(x.shape) >= LANES - step, after, rolled)


def from_left(x, step):
    rolled = pltpu.roll(x, step, x.ndim - 1)
    if x.shape[1] == 1:
        return rolled
    before = jnp.concatenate([rolled[:, -1:], rolled[:, :-1]], axis=1)
    return jnp.where(lane_iota(x.shape) < step, before, rolled)


def weight(kx, kx_lo, ky, kz, surf, step):
    diag = surf + kx + kx_lo + ky + from_left(ky, step) + kz
    return jnp.where(diag > 0.0, damping / jnp.where(diag > 0.0, diag, 1.0), 0.0)


def residual_of(f, u, u_up, u_dn, kx, kx_lo, ky, kz, surf, step):
    flux = ky * (u - from_right(u, step))
    vert = kz * (u[0:1] - u[1:2])
    out = surf * u + kx * (u - u_up) + kx_lo * (u - u_dn)
    out = out + flux - from_left(flux, step)
    return f - (out + jnp.concatenate([vert, -vert], axis=0))


def lane_take(x, index):
    parts = [
        jnp.take_along_axis(x[r : r + 8], index[r : r + 8], axis=1, mode="promise_in_bounds")
        for r in range(0, x.shape[0], 8)
    ]
    return parts[0] if len(parts) == 1 else jnp.concatenate(parts, axis=0)


def row_take(x, index):
    parts = [
        jnp.take_along_axis(x[r : r + 8], index[r : r + 8], axis=0, mode="promise_in_bounds")
        for r in range(0, x.shape[0], 8)
    ]
    return parts[0] if len(parts) == 1 else jnp.concatenate(parts, axis=0)


def rows_of(ref, plane, count, start, size=8):
    return ref[plane : plane + count, :, start : start + size, :]


def block_residual(level, u_ref, u_at, step, r0):
    u = rows_of(u_ref, u_at, 2, r0)
    return u, residual_of(
        rows_of(level, F, 2, r0),
        u,
        rows_of(u_ref, u_at, 2, r0 + 1),
        rows_of(u_ref, u_at, 2, r0 - 1),
        rows_of(level, KX, 2, r0),
        rows_of(level, KX, 2, r0 - 1),
        rows_of(level, KY, 2, r0),
        rows_of(level, KZ, 1, r0),
        rows_of(level, S, 2, r0),
        step,
    )


def put(ref, plane, r0, value):
    ref[plane : plane + value.shape[0], :, r0 : r0 + value.shape[2], :] = value


def strided(ref, plane, count, start, size):
    tiles = ref.shape[1]
    return jnp.stack(
        [
            jnp.stack([ref[plane + p, c, pl.ds(start, size, stride=2), :] for c in range(tiles)])
            for p in range(count)
        ]
    )


def put_strided(ref, plane, start, value):
    for p in range(value.shape[0]):
        for c in range(value.shape[1]):
            ref[plane + p, c, pl.ds(start, value.shape[2], stride=2), :] = value[p, c]


def coarse_block(fine, resid, step, fine_row, size):
    def both(ref, plane, count):
        return strided(ref, plane, count, fine_row, size) + strided(
            ref, plane, count, fine_row + 1, size
        )

    f = both(resid, 0, 2)
    kx = strided(fine, KX, 2, fine_row + 1, size)
    ky = both(fine, KY, 2)
    surf_kz = both(fine, S, 3)
    summed = jnp.concatenate([f, kx, surf_kz], axis=0)
    summed = summed + from_right(summed, step)
    return summed[0:2], summed[2:4], from_right(ky, step), summed[4:7]


def blocks(own, count, halo):
    more = -(-halo // 8) * 8
    return range(own - more, own + count + more, 8)


def sides(mine, other, is_even):
    low = jnp.where(is_even, other, mine)
    high = jnp.where(is_even, mine, other)
    return low, high


def sides_x(near, far):
    me = lax.axis_index("gx")
    low, high = sides(near, far, lax.rem(me, 2) == 0)
    return jnp.where(me == 0, 0.0, low), high


def pack_kernel(source, coef_x, coef_y, surface, coef_z, out, c_ref, d_ref, sems):
    inputs = ((source, F, 2), (coef_x, KX, 2), (coef_y, KY, 2), (surface, S, 2), (coef_z, KZ, 0))
    copies = []
    for k, (ref, plane, count) in enumerate(inputs):
        to = out.at[plane : plane + count] if count else out.at[plane]
        copies.append(pltpu.make_async_copy(ref, to, sems.at[k]))
    for copy in copies:
        copy.start()
    for copy in copies:
        copy.wait()
    rows, cols = out.shape[1], out.shape[2]
    wall_x = lax.axis_index("gx") == lax.axis_size("gx") - 1
    wall_y = lax.axis_index("gy") == lax.axis_size("gy") - 1
    edge = out[KX : KX + 2, rows - 8 :, :]
    row = lax.broadcasted_iota(jnp.int32, edge.shape, 1)
    out[KX : KX + 2, rows - 8 :, :] = jnp.where(wall_x & (row == 7), 0.0, edge)
    edge = out[KY : KY + 2, :, cols - LANES :]
    out[KY : KY + 2, :, cols - LANES :] = jnp.where(
        wall_y & (lane_iota(edge.shape) == LANES - 1), 0.0, edge
    )

    even_y = lax.rem(lax.axis_index("gy"), 2) == 0
    lane = lane_iota((8, LANES))
    for r0 in range(0, rows, 8):
        left = [jnp.zeros((8, LANES), jnp.float32)] * 2
        right = list(left)
        for p in range(PLANES):
            begin = p * WIDTH
            for tiles, column, offset in ((left, 0, 0), (right, cols - LANES, LANES - WIDTH)):
                piece = out[p, r0 : r0 + 8, column : column + LANES]
                rolled = pltpu.roll(piece, (begin - offset) % LANES, 1)
                for a in range(2):
                    lo, hi = begin - a * LANES, begin + WIDTH - a * LANES
                    if hi > 0 and lo < LANES:
                        tiles[a] = jnp.where((lane >= lo) & (lane < hi), rolled, tiles[a])
        for a in range(2):
            at = (slice(r0, r0 + 8), slice(a * LANES, (a + 1) * LANES))
            c_ref[at] = jnp.where(even_y, right[a], left[a])
            d_ref[at] = jnp.where(even_y, left[a], right[a])


def down_kernel(
    own_ref, near_ref, far_ref, own_cd, near_cd, far_cd, l0, l1, l2, pack_ref, ua, rr, row9
):
    even_y = lax.rem(lax.axis_index("gy"), 2) == 0
    rows = own_ref.shape[1]
    lane = lane_iota((8, LANES))

    def take(tiles, p, offset):
        begin = p * WIDTH
        a, b = begin // LANES, (begin + WIDTH - 1) // LANES
        piece = tiles[a]
        if a != b:
            piece = jnp.where(lane < begin + WIDTH - b * LANES, tiles[b], tiles[a])
        return pltpu.roll(piece, (offset - begin) % LANES, 1)

    for block in range(3 * rows // 8):
        part, r0 = divmod(block * 8, rows)
        to = slice(PAD + block * 8, PAD + block * 8 + 8)
        for p in range(PLANES):
            for c in range(2):
                at = (p, slice(r0, r0 + 8), slice(c * LANES, (c + 1) * LANES))
                if part == 1:
                    l0[p, c, to, :] = own_ref[at]
                else:
                    l0[p, c, to, :] = sides_x(near_ref[at], far_ref[at])[part // 2]
        low, high = [], []
        for a in range(2):
            held = []
            for base in (rows, 0):
                at = (slice(base + r0, base + r0 + 8), slice(a * LANES, (a + 1) * LANES))
                if part == 1:
                    held.append(own_cd[at])
                else:
                    held.append(sides_x(near_cd[at], far_cd[at])[part // 2])
            lo, hi = sides(held[0], held[1], even_y)
            low.append(lo)
            high.append(hi)
        for p in range(PLANES):
            right = take(high, p, 0)
            left = take(low, p, LANES - WIDTH)
            l0[p, 2, to, :] = jnp.where(
                lane < WIDTH, right, jnp.where(lane >= LANES - WIDTH, left, 0.0)
            )

    halos = ((26, 25, 24), (12, 11, 10), (5, 4, 0))
    levels = (l0, l1, l2)
    for depth, level in enumerate(levels):
        step = 1 << depth
        count = (level.shape[2] - 2 * PAD) // 3
        first, second, last = (blocks(PAD + count, count, halo) for halo in halos[depth])
        if depth:
            for r0 in range(PAD, PAD + 3 * count, 8):
                f, kx, ky, surf_kz = coarse_block(
                    levels[depth - 1], rr, step // 2, PAD + 2 * (r0 - PAD), 8
                )
                put(level, F, r0, f)
                put(level, KX, r0, kx)
                put(level, KY, r0, ky)
                put(level, S, r0, surf_kz)
        for r0 in first:
            w = weight(
                rows_of(level, KX, 2, r0),
                rows_of(level, KX, 2, r0 - 1),
                rows_of(level, KY, 2, r0),
                rows_of(level, KZ, 1, r0),
                rows_of(level, S, 2, r0),
                step,
            )
            put(level, W, r0, w)
            put(ua, 0, r0, w * rows_of(level, F, 2, r0))
        for r0 in second:
            u, r = block_residual(level, ua, 0, step, r0)
            put(level, U, r0, u + rows_of(level, W, 2, r0) * r)
        for r0 in last:
            put(rr, 0, r0, block_residual(level, level, U, step, r0)[1])

    own = l2.shape[2] // 2 - 4
    f, kx, ky, surf_kz = coarse_block(l2, rr, 4, own, 8)
    nine = jnp.concatenate([f, kx, ky, surf_kz], axis=0)
    place = lax.broadcasted_iota(jnp.int32, (8, LANES), 0)
    cell = lane % 32
    index = cell * 8 % LANES
    mine = place == (lane // 32 + lax.axis_index("gy")) % 4
    total = jnp.zeros((PLANES, LANES), jnp.float32)
    for r in range(4):
        src = lax.broadcasted_iota(jnp.int32, (2 * LANES, LANES), 0)
        dst = lax.broadcasted_iota(jnp.int32, (2 * LANES, LANES), 1)
        group = (dst // 32 + lax.axis_index("gy")) % 4
        pick = jnp.where((src == dst % 32 * 8) & (group == r), 1.0, 0.0)
        total = total + jnp.dot(
            jnp.concatenate([nine[:, 0, r, :], nine[:, 1, r, :]], axis=1),
            pick,
            precision=lax.Precision.HIGHEST,
            preferred_element_type=jnp.float32,
        )
    row9[0:PLANES] = total
    row9[PLANES : 2 * PLANES] = total
    for r0 in range(0, pack_ref.shape[0], 8):
        pack_ref[r0 : r0 + 8] = row9[r0 % PLANES : r0 % PLANES + 8]


def scaled(level, weights, step):
    f, kx, kx_lo, ky, kz, surf = level
    faces = (f, kx, kx_lo, ky, from_left(ky, step), kz)
    return tuple(weights * x for x in faces)


def whole_sweep(faces, u, step):
    f, up, down, right, left, across = faces
    rows = u.shape[2]
    other = jnp.concatenate([u[1:2], u[0:1]], axis=0)
    near = ((1.0 - damping) * u + f) + across * other
    along = up * pltpu.roll(u, rows - 1, 2) + down * pltpu.roll(u, 1, 2)
    return near + along + (right * from_right(u, step) + left * from_left(u, step))


def whole_residual(level, u, step):
    f, kx, kx_lo, ky, kz, surf = level
    rows = u.shape[2]
    return residual_of(
        f, u, pltpu.roll(u, rows - 1, 2), pltpu.roll(u, 1, 2), kx, kx_lo, ky, kz, surf, step
    )


def up_kernel(nx, ny, x_ref, l0, l1, l2, p_ref, r_ref, g3, g4, g5, ub, uc, p_own, r_own, sems):
    me_x = lax.axis_index("gx")
    me_y = lax.axis_index("gy")
    tiles = ny // 4
    rows3 = nx * 4

    lane = lane_iota((rows3, LANES))
    row = lax.broadcasted_iota(jnp.int32, (rows3, LANES), 0)
    to_row = row % 8 // 4 * 4 + (row - lane // 32 + 4) % 4
    to_lane = (row - lane // 32 + 4) % 4 * 32 + lane % 32
    for p in range(PLANES):
        for q in range(tiles):
            if tiles == 1:
                x = x_ref[pl.ds(p, rows3, stride=PLANES), :]
            else:
                x = jnp.concatenate(
                    [
                        x_ref[pl.ds((i * ny + 4 * q) * PLANES + p, 4, stride=PLANES), :]
                        for i in range(nx)
                    ],
                    axis=0,
                )
            out = lane_take(row_take(x, to_row), to_lane)
            g3[p, q, :, :] = out

    def gathered(ref):
        kx = ref[KX : KX + 2]
        return (
            ref[F : F + 2],
            kx,
            pltpu.roll(kx, 1, 2),
            ref[KY : KY + 2],
            ref[KZ : KZ + 1],
            ref[S : S + 2],
        )

    level3 = gathered(g3)
    w3 = weight(*level3[1:], 1)
    faces3 = scaled(level3, w3, 1)
    u3 = whole_sweep(faces3, faces3[0], 1)
    g4[0:2] = whole_residual(level3, u3, 1)
    f, kx, ky, surf_kz = coarse_block(g3, g4, 1, 0, rows3 // 2)
    level4 = (f, kx, pltpu.roll(kx, 1, 2), ky, surf_kz[2:3], surf_kz[0:2])
    w4 = weight(*level4[1:], 2)
    faces4 = scaled(level4, w4, 2)
    u4 = faces4[0]
    for sweep in range(CSWEEPS - 1):
        u4 = whole_sweep(faces4, u4, 2)
    rc = whole_residual(level4, u4, 2)
    even = lane_iota(u4.shape) % 2 == 0

    def total(x):
        x = jnp.sum(jnp.where(even, x, 0.0), axis=(0, 1))
        return jnp.sum(jnp.sum(x, axis=0, keepdims=True), axis=1, keepdims=True)

    shift = (total(rc) / total(level4[5]))[None, None]
    spread4 = jnp.where(even, u4, from_left(u4, 1))
    put_strided(g4, 0, 0, spread4)
    put_strided(g4, 0, 1, spread4)
    u3 = (u3 + g4[0:2]) + shift
    for sweep in range(POST):
        u3 = whole_sweep(faces3, u3, 1)

    rows2 = l2.shape[2] - 2 * PAD
    margin = jnp.zeros((2, tiles, PAD, LANES), jnp.float32)
    g5[:, :, 0:PAD] = margin
    g5[:, :, PAD : PAD + rows3] = u3
    g5[:, :, PAD + rows3 : 2 * PAD + rows3] = margin
    lane = lane_iota((8, LANES))
    first = me_x * 4 + PAD - 2
    skip = rows2 // 2 - 8
    for k in range(2):
        near = [g5[k, q, pl.ds(first, 8), :] for q in range(tiles)]
        for c in range(3):
            column = lane + c * LANES
            column = jnp.where(column >= 320, column - 384, column)
            coarse = (column + 64) // 8 - 8 + me_y * 32 + LANES
            index = coarse % LANES
            spread = lane_take(near[0], index)
            for q in range(1, tiles):
                spread = jnp.where(coarse // LANES == q + 1, lane_take(near[q], index), spread)
            for at in (PAD + skip, PAD + skip + 1):
                uc[k, c, pl.ds(at, 8, stride=2), :] = spread

    levels = (l0, l1, l2)
    for depth in (2, 1, 0):
        level = levels[depth]
        step = 1 << depth
        count = (level.shape[2] - 2 * PAD) // 3
        own = PAD + count
        starts = blocks(own, count, 4)
        for r0 in starts:
            put(uc, 0, r0, rows_of(uc, 0, 2, r0) + rows_of(level, U, 2, r0))
        for source, target in ((uc, ub), (ub, uc)):
            for r0 in starts:
                u, r = block_residual(level, source, 0, step, r0)
                put(target, 0, r0, u + rows_of(level, W, 2, r0) * r)
        if depth:
            half = step // 2
            finer = PAD + 2 * count - 4
            spread = []
            for r0 in range(own - 2, own + count + 2, 4):
                e = rows_of(uc, 0, 2, r0, 4)
                spread.append(
                    jnp.where(lane_iota(e.shape) % step < half, e, from_left(e, half))
                )
            for k, e in enumerate(spread):
                put_strided(ub, 0, finer + 8 * k, e)
                put_strided(ub, 0, finer + 8 * k + 1, e)
            for k in range(len(spread)):
                put(uc, 0, finer + 8 * k, rows_of(ub, 0, 2, finer + 8 * k))
        else:
            for r0 in range(0, count, 8):
                u = rows_of(uc, 0, 2, own + r0)
                for c in range(2):
                    p_own[:, r0 : r0 + 8, c * LANES : (c + 1) * LANES] = u[:, c]
            copy_p = pltpu.make_async_copy(p_own, p_ref, sems.at[0])
            copy_p.start()
            for r0 in range(0, count, 8):
                r = block_residual(level, uc, 0, step, own + r0)[1]
                for c in range(2):
                    r_own[:, r0 : r0 + 8, c * LANES : (c + 1) * LANES] = r[:, c]
            copy_r = pltpu.make_async_copy(r_own, r_ref, sems.at[1])
            copy_r.start()
            copy_p.wait()
            copy_r.wait()


def shape_of(*shape):
    return jax.ShapeDtypeStruct(shape, jnp.float32)


def vmem(*shape):
    return pltpu.VMEM(shape, jnp.float32)


def on_device(source, coef_x, coef_y, coef_z, surface):
    rows, cols = source.shape[1], source.shape[2]
    nx, ny = lax.axis_size("gx"), lax.axis_size("gy")
    params = pltpu.CompilerParams(vmem_limit_bytes=24 * 1024 * 1024)
    packed, strip_c, strip_d = pl.pallas_call(
        pack_kernel,
        out_shape=(shape_of(PLANES, rows, cols),) + (shape_of(rows, 2 * LANES),) * 2,
        in_specs=[pl.BlockSpec(memory_space=pltpu.HBM)] * 5,
        scratch_shapes=[pltpu.SemaphoreType.DMA((5,))],
        compiler_params=params,
        name="pack",
    )(
        *(
            pltpu.with_memory_space_constraint(x, pltpu.HBM)
            for x in (source, coef_x, coef_y, surface, coef_z)
        )
    )

    strip_c = pair_permute(strip_c, "gy", 0)
    strip_d = pair_permute(strip_d, "gy", 1, wrap=True)
    far = far_permute(packed)
    near = pair_permute(packed, "gx", 0)
    strips = jnp.concatenate([strip_d, strip_c], axis=0)
    nil = 0.0 * lax.axis_index("gy").astype(jnp.float32)
    strips = lax.optimization_barrier(strips) + nil
    far_strips = far_permute(strips)
    near_strips = pair_permute(strips, "gx", 0)

    heights = [3 * rows // (1 << depth) + 2 * PAD for depth in range(3)]
    planes = U + 2
    l0, l1, l2, pack = pl.pallas_call(
        down_kernel,
        out_shape=tuple(shape_of(planes, 3, h, LANES) for h in heights)
        + (shape_of(nx * ny * PLANES, LANES),),
        scratch_shapes=[vmem(2, 3, heights[0], LANES)] * 2 + [vmem(24, LANES)],
        compiler_params=params,
        name="down",
    )(packed, near, far, strips, near_strips, far_strips)

    everyone = lax.all_to_all(
        pack.reshape(nx * ny, 1, PACK), ("gx", "gy"), 0, 0, tiled=True
    )
    everyone = everyone.reshape(nx * ny * PLANES, LANES)

    tiles = ny // 4
    pressure, residual = pl.pallas_call(
        functools.partial(up_kernel, nx, ny),
        out_shape=(shape_of(*source.shape),) * 2,
        scratch_shapes=[
            vmem(PLANES, tiles, nx * 4, LANES),
            vmem(2, tiles, nx * 4, LANES),
            vmem(2, tiles, nx * 4 + 2 * PAD, LANES),
            vmem(2, 3, heights[0], LANES),
            vmem(2, 3, heights[0], LANES),
            vmem(*source.shape),
            vmem(*source.shape),
            pltpu.SemaphoreType.DMA((2,)),
        ],
        out_specs=[pl.BlockSpec(memory_space=pltpu.HBM)] * 2,
        compiler_params=params,
        name="up",
    )(everyone, l0, l1, l2)
    return pressure, residual


def solution(mesh):
    layered, plane = P(None, "gx", "gy"), P("gx", "gy")
    return jax.shard_map(
        on_device,
        mesh=mesh,
        in_specs=(layered, layered, layered, plane, layered),
        out_specs=(layered, layered),
        check_vma=False,
    )
```
